256 devices in a mesh: ctx: 64 (over y, x_lo, z), head: 4 (over x_hi, core).
Axes of the slice: x: 4 (x_hi: 2, x_lo: 2; x = x_hi * 2 + x_lo), y: 4, z: 8, core: 2. Of those that a mesh axis runs over, the one named last changes fastest.
Arguments:
- queries: bfloat16 [32768, 4, 512], P('ctx', 'head'), may hold values from -5 to 5
- keys: bfloat16 [32768, 512], P('ctx'), may hold values from -5 to 5
- values: bfloat16 [32768, 512], P('ctx'), may hold values from -5 to 5
- grad_out: bfloat16 [32768, 4, 512], P('ctx', 'head'), may hold values from -24 to 24
- doc_lengths: int32 [64], replicated, may hold values from 1 to 1024, 32768 in all
Outputs:
- query_grad: bfloat16 [32768, 4, 512], P('ctx', 'head')
- key_grad: bfloat16 [32768, 512], P(('ctx', 'head'))
- value_grad: bfloat16 [32768, 512], P(('ctx', 'head'))
The draws below stay inside these ranges and needn't reach their ends.
Inputs may be any that keep to these rules, and one draw needn't show every extreme that they name: `doc_lengths`: documents packed one after another; the lengths sum to 32768 and the longest has exactly 1024 tokens.
All inputs are finite; a program needn't handle non-finite values.
Results may differ from the reference program's by a relative error of at most 0.011.
Values may be sent and summed in bfloat16 or wider, within the bound.
A program may use at most 64 MiB of HBM per device.

```python
import math
import jax
import jax.numpy as jnp
import numpy as np
from jax import lax

HD = 128
GROUP = 4
KVH = 4
TOK_DEV = 512
HOPS = 2
SEQ = 32768
DOC_MAX = 1024
NDOCS = 64


def draw_queries(key, part):
    shape = (SEQ, GROUP, KVH * HD)
    base = jnp.clip(jax.random.normal(jax.random.fold_in(key, 1), shape, jnp.float32), -4.5, 4.5)
    return base.astype(jnp.bfloat16)


def draw_keys(key, part):
    shape = (SEQ, KVH * HD)
    base = jnp.clip(jax.random.normal(jax.random.fold_in(key, 2), shape, jnp.float32), -4.5, 4.5)
    return base.astype(jnp.bfloat16)


def steps_of(rng, shape, split, smallest, top_value):
    factor_of, own = 1.0, jax.random.fold_in(rng, 6)
    for dim, shards_of in split:
        draws = jnp.exp(jax.random.uniform(jax.random.fold_in(own, dim), (shards_of,), jnp.float32, smallest / len(split), top_value / len(split)))
        factor_of = factor_of * jnp.repeat(draws, shape[dim] // shards_of).reshape([-1 if axis == dim else 1 for axis in range(len(shape))])
    return factor_of


def profile(number_of, total, reach, skew):
    weights = [(1 << 20) // math.isqrt(standing ** skew) + 1 for standing in range(2, number_of + 1)]
    surplus, given = total - reach - (number_of - 1), [1] * (number_of - 1)
    while surplus > 0:
        movable = [i for i in range(number_of - 1) if given[i] < reach]
        pool, budget = sum([weights[i] for i in movable]), surplus
        for i in movable:
            extra = min(reach - given[i], max(1, budget * weights[i] // pool), surplus)
            given[i] = given[i] + extra
            surplus = surplus - extra
    return np.array([reach] + given)


def uneven(key, count, total, bound, slope):
    if count == 2:
        one = jax.random.randint(key, (), max(1, total - bound), min(bound, total - 1) + 1)
        return jnp.stack([one, total - one])
    tallies = jnp.asarray(profile(count, total, bound, slope), jnp.int32)
    twos = (count - 1) // 2
    giver, taker = tallies[1:1 + 2 * twos:2], tallies[2:2 + 2 * twos:2]
    room = jnp.minimum(giver - 1, bound - taker)
    shifted = jax.random.randint(jax.random.fold_in(key, 1), (twos,), 0, 1 << 20) % (room + 1)
    tallies = tallies.at[1:1 + 2 * twos:2].set(giver - shifted).at[2:2 + 2 * twos:2].set(taker + shifted)
    return tallies[jax.random.permutation(jax.random.fold_in(key, 2), count)]


def bell_draw(stream_key, dims, spread, reach, cuts=(), kind=jnp.bfloat16):
    result = spread * jax.random.normal(stream_key, dims, jnp.float32)
    if cuts:
        result = result * steps_of(stream_key, dims, cuts, -0.22, 0.18)
    return jnp.clip(result, -reach, reach).astype(kind)


def setup_inputs(seed: int = 0) -> dict:
    key_list = jax.random.split(jax.random.key(seed), 6)
    return {
        "queries": draw_queries(jax.random.fold_in(key_list[5], 71), 0),
        "keys": draw_keys(jax.random.fold_in(key_list[5], 71), 0),
        "values": bell_draw(key_list[2], (SEQ, KVH * HD), 1.0, 5.0, ((0, 64),)),
        "grad_out": bell_draw(key_list[3], (SEQ, GROUP, KVH * HD), 4.0, 24.0, ((0, 64), (1, 4))),
        "doc_lengths": uneven(key_list[4], NDOCS, SEQ, DOC_MAX, 2).astype(jnp.int32),
    }


def doc_index(doc_lengths, positions):
    doc_ends = jnp.cumsum(doc_lengths).astype(jnp.int32)
    return lax.optimization_barrier(jnp.sum((doc_ends[None, :] <= positions[:, None]).astype(jnp.int32), axis=1)).astype(jnp.int32)

def reference(queries, keys, values, grad_out, doc_lengths):
    reach_rows = HOPS * TOK_DEV
    window_rows = reach_rows + TOK_DEV
    score_scale = 1.0 / math.sqrt(HD)
    lead_zeros = jnp.zeros((reach_rows, KVH * HD), keys.dtype)
    padded_keys = jnp.concatenate([lead_zeros, keys], axis=0)
    padded_values = jnp.concatenate([lead_zeros, values], axis=0)
    local_rows = jnp.arange(TOK_DEV, dtype=jnp.int32)
    window_offsets = jnp.arange(window_rows, dtype=jnp.int32)

    def one_block(totals, block_index):
        key_grads, value_grads = totals
        row_start = (block_index * TOK_DEV).astype(jnp.int32)
        q_block = lax.dynamic_slice_in_dim(queries, row_start, TOK_DEV, 0).astype(jnp.float32).reshape(TOK_DEV, GROUP, KVH, HD)
        g_block = lax.dynamic_slice_in_dim(grad_out, row_start, TOK_DEV, 0).astype(jnp.float32).reshape(TOK_DEV, GROUP, KVH, HD)
        k_window = lax.dynamic_slice_in_dim(padded_keys, row_start, window_rows, 0).astype(jnp.float32).reshape(window_rows, KVH, HD)
        v_window = lax.dynamic_slice_in_dim(padded_values, row_start, window_rows, 0).astype(jnp.float32).reshape(window_rows, KVH, HD)
        q_pos = row_start + local_rows
        k_pos = row_start - reach_rows + window_offsets
        same_doc = doc_index(doc_lengths, k_pos)[None, :] == doc_index(doc_lengths, q_pos)[:, None]
        allowed = (k_pos[None, :] <= q_pos[:, None]) & (k_pos[None, :] >= 0) & same_doc
        raw_scores = jnp.einsum('tmgd,ugd->mgtu', q_block, k_window) * score_scale
        raw_scores = jnp.where(allowed[None, None], raw_scores, -jnp.inf)
        row_top = lax.optimization_barrier(jnp.max(raw_scores, axis=-1, keepdims=True))
        log_norm = row_top + jnp.log(lax.optimization_barrier(jnp.sum(jnp.exp(raw_scores - row_top), axis=-1, keepdims=True)))
        weights = jnp.exp(raw_scores - log_norm)
        weights_b = lax.optimization_barrier(weights.astype(jnp.bfloat16)).astype(jnp.float32)
        attn_out = jnp.einsum('mgtu,ugd->tmgd', weights_b, v_window)
        row_delta = jnp.einsum('tmgd,tmgd->mgt', g_block, attn_out)
        weight_grads = jnp.einsum('tmgd,ugd->mgtu', g_block, v_window)
        score_grads = weights * (weight_grads - row_delta[..., None]) * score_scale
        score_grads = lax.optimization_barrier(score_grads.astype(jnp.bfloat16)).astype(jnp.float32)
        query_grads = jnp.einsum('mgtu,ugd->tmgd', score_grads, k_window)
        key_part = jnp.einsum('mgtu,tmgd->ugd', score_grads, q_block).reshape(window_rows, KVH * HD)
        value_part = jnp.einsum('mgtu,tmgd->ugd', weights_b, g_block).reshape(window_rows, KVH * HD)
        key_grads = lax.dynamic_update_slice_in_dim(key_grads, lax.dynamic_slice_in_dim(key_grads, row_start, window_rows, 0) + key_part, row_start, 0)
        value_grads = lax.dynamic_update_slice_in_dim(value_grads, lax.dynamic_slice_in_dim(value_grads, row_start, window_rows, 0) + value_part, row_start, 0)
        return ((key_grads, value_grads), query_grads.reshape(TOK_DEV, GROUP, KVH * HD).astype(jnp.bfloat16))
    empty_grads = jnp.zeros((SEQ + reach_rows, KVH * HD), jnp.float32)
    block_count = SEQ // TOK_DEV
    finals, query_blocks = lax.scan(one_block, (empty_grads, empty_grads), jnp.arange(block_count, dtype=jnp.int32))
    query_grad = query_blocks.reshape(SEQ, GROUP, KVH * HD)
    key_grad = finals[0][reach_rows:].astype(jnp.bfloat16)
    value_grad = finals[1][reach_rows:].astype(jnp.bfloat16)
    return (query_grad, key_grad, value_grad)
```

```python
import math

import jax
import jax.numpy as jnp
from jax import lax
from jax.experimental import pallas as pl
from jax.experimental.pallas import tpu as pltpu
from jax.sharding import PartitionSpec as P

HD = 128
KVH = 4
TOK = 512
HALF = 256
REACH = 1024
WIN = REACH + TOK
SPAN = REACH + HALF
STAGES = 2
MESH = pl.DeviceIdType.MESH
SCALE = 1.0 / math.sqrt(HD)
LOG2E = math.log2(math.e)
NT = (((1,), (1,)), ((), ()))
TN = (((0,), (0,)), ((), ()))


def mm(a, b):
    return jnp.dot(a, b, preferred_element_type=jnp.float32)


def kernel(
    ctx_size,
    q_ref, k_ref, v_ref, g_ref, len_ref,
    dq_ref, dk_ref, dv_ref,
    win, qo, pd, mine, dqs, begin,
    mate_out, mate_in, hop1, hop0, r2_out, r2_in, r1_out, r1_in, fin,
    load_sem, z1_s, z1_r, z2_s, z2_r, m1_s, m1_r, m2_s, m2_r, x_s, x_r,
    mt_s, mt_r, r2_s, r2_r, r1_s, r1_r, dq_s, dq_r, dq_l, f_s, f_r, f_l,
):
    ctx = lax.axis_index("ctx")
    head = lax.axis_index("head")
    core = lax.rem(head, 2)
    chip = head // 2
    other = 1 - core
    nxt = (lax.rem(ctx + 1, ctx_size), head)
    prv = (lax.rem(ctx + ctx_size - 1, ctx_size), head)
    mate = (ctx, chip * 2 + other)
    partner = (ctx, (1 - chip) * 2 + core)
    diagonal = (ctx, (1 - chip) * 2 + other)

    def cols(owner, s):
        return pl.ds(pl.multiple_of((owner * 2 + s) * HD, HD), HD)

    def remote(src, dst, send, recv, device):
        return pltpu.make_async_remote_copy(
            src_ref=src, dst_ref=dst, send_sem=send, recv_sem=recv,
            device_id=device, device_id_type=MESH,
        )

    own_rows = pl.ds(REACH, TOK)
    hop1_rows = pl.ds(TOK, TOK)
    hop2_rows = pl.ds(0, TOK)

    loads = []
    for s in range(STAGES):
        for kind, ref in ((0, k_ref), (1, v_ref)):
            loads.append(pltpu.make_async_copy(
                ref.at[:, cols(chip, s)], win.at[kind, s, own_rows], load_sem.at[kind, s]))
        for kind, ref in ((0, q_ref), (1, g_ref)):
            loads.append(pltpu.make_async_copy(
                ref.at[:, :, cols(chip, s)], qo.at[kind, s, :, 0], load_sem.at[2 + kind, s]))
    for load in loads:
        load.start()

    barrier = pltpu.get_barrier_semaphore()
    for device in (nxt, prv, mate, partner, diagonal):
        pl.semaphore_signal(barrier, 1, device_id=device, device_id_type=MESH)

    lengths = jnp.broadcast_to(len_ref[...], (64, 64)).astype(jnp.float32)
    upto = lax.broadcasted_iota(jnp.int32, (64, 64), 1) <= lax.broadcasted_iota(jnp.int32, (64, 64), 0)
    ends = jnp.sum(jnp.where(upto, lengths, 0.0), axis=1, keepdims=True).astype(jnp.int32)
    pos = lax.broadcasted_iota(jnp.int32, (64, TOK), 1) + ctx * TOK
    first = jnp.max(jnp.where(ends <= pos, ends, 0), axis=0, keepdims=True)
    begin[...] = jnp.broadcast_to(first - ctx * TOK + REACH, (8, TOK))

    for load in loads:
        load.wait()
    pl.semaphore_wait(barrier, 5)

    z1 = [remote(win.at[core, s, own_rows], win.at[core, s, hop1_rows], z1_s.at[s], z1_r.at[s], nxt)
          for s in range(STAGES)]
    z2 = [remote(win.at[core, s, hop1_rows], win.at[core, s, hop2_rows], z2_s.at[s], z2_r.at[s], nxt)
          for s in range(STAGES)]
    m1 = [remote(win.at[core, s, hop1_rows], win.at[core, s, hop1_rows], m1_s.at[s], m1_r.at[s], mate)
          for s in range(STAGES)]
    m1_in = [remote(win.at[other, s, hop1_rows], win.at[other, s, hop1_rows], m1_s.at[s], m1_r.at[s], mate)
             for s in range(STAGES)]
    m2 = [remote(win.at[core, s, hop2_rows], win.at[core, s, hop2_rows], m2_s.at[s], m2_r.at[s], mate)
          for s in range(STAGES)]
    m2_in = [remote(win.at[other, s, hop2_rows], win.at[other, s, hop2_rows], m2_s.at[s], m2_r.at[s], mate)
             for s in range(STAGES)]
    xq = [[remote(ref.at[:, :, cols(1 - chip, s)], qo.at[kind, s, :, 1], x_s.at[kind, s], x_r.at[kind, s], partner)
           for kind, ref in ((0, q_ref), (1, g_ref))] for s in range(STAGES)]
    mt = [remote(mate_out.at[s], mate_in.at[s], mt_s.at[s], mt_r.at[s], mate) for s in range(STAGES)]
    r2 = [remote(r2_out.at[s], r2_in.at[s], r2_s.at[s], r2_r.at[s], prv) for s in range(STAGES)]
    r1 = [remote(r1_out.at[s], r1_in.at[s], r1_s.at[s], r1_r.at[s], prv) for s in range(STAGES)]
    dq_far = [remote(dqs.at[s, 1], dq_ref.at[:, :, cols(chip, s)], dq_s.at[s], dq_r.at[s], partner)
              for s in range(STAGES)]
    dq_far_in = [remote(dqs.at[s, 1], dq_ref.at[:, :, cols(1 - chip, s)], dq_s.at[s], dq_r.at[s], partner)
                 for s in range(STAGES)]
    dq_near = [pltpu.make_async_copy(dqs.at[s, 0], dq_ref.at[:, :, cols(chip, s)], dq_l.at[s])
               for s in range(STAGES)]

    z1[0].start()
    for copy in xq[0]:
        copy.start()
    z1[1].start()
    for copy in xq[1]:
        copy.start()
    z1[0].wait_recv()
    z2[0].start()
    m1[0].start()

    causal = (lax.broadcasted_iota(jnp.int32, (HALF, HALF), 0)
              <= lax.broadcasted_iota(jnp.int32, (HALF, HALF), 1))
    place = lax.broadcasted_iota(jnp.int32, (SPAN, HALF), 0)

    def unit(s, c, j):
        rows = pl.ds(c * HALF, SPAN)
        k_win = win[0, s, rows]
        scores = lax.dot_general(k_win, qo[0, s, c, j], NT, preferred_element_type=jnp.float32)
        lowest = begin[0:1, c * HALF:(c + 1) * HALF] - c * HALF
        scores = jnp.where(place >= lowest, scores, -1e30)
        scores = jnp.concatenate(
            [scores[:REACH], jnp.where(causal, scores[REACH:], -1e30)], axis=0)
        top = jnp.max(scores, axis=0, keepdims=True)
        weights = jnp.exp2((scores - top) * (SCALE * LOG2E))
        inverse = 1.0 / jnp.sum(weights, axis=0, keepdims=True)
        grads = lax.dot_general(win[1, s, rows], qo[1, s, c, j], NT, preferred_element_type=jnp.float32)
        delta = jnp.sum(weights * grads, axis=0, keepdims=True) * inverse
        at = pl.ds(c * TOK + j * HALF, HALF)
        pd[1, rows, at] = (weights * inverse).astype(jnp.bfloat16)
        score_grads = (weights * (grads - delta) * (inverse * SCALE)).astype(jnp.bfloat16)
        pd[0, rows, at] = score_grads
        dqs[s, j, c] = lax.dot_general(
            score_grads, k_win, TN, preferred_element_type=jnp.float32).astype(jnp.bfloat16)

    pieces = ((0, HALF, 0, 1), (HALF, SPAN, 0, 2), (SPAN, WIN, 1, 2))

    def product(kind, s, piece):
        low, high, c0, c1 = piece
        right = qo[kind, s, c0:c1].reshape(((c1 - c0) * TOK, HD))
        return mm(pd[kind, low:high, c0 * TOK:c1 * TOK], right)

    def finish(s):
        r1[s].wait_recv()
        fin[s] = (hop0[s] + r1_in[s].astype(jnp.float32)).astype(jnp.bfloat16)
        for which, out in ((0, dk_ref), (1, dv_ref)):
            @pl.when(core == which)
            def _(out=out):
                for step, device in enumerate((partner, diagonal, mate)):
                    block = pl.ds(pl.multiple_of(device[1] * 128, 128), 128)
                    remote(fin.at[s, block], out.at[:, cols(chip, s)],
                           f_s.at[s, step], f_r.at[s, step], device).start()
                block = pl.ds(pl.multiple_of(head * 128, 128), 128)
                pltpu.make_async_copy(fin.at[s, block], out.at[:, cols(chip, s)], f_l.at[s]).start()

    def middle(s):
        r2[s].wait_recv()
        r1_out[s] = (hop1[s] + r2_in[s].astype(jnp.float32)).astype(jnp.bfloat16)
        r1[s].start()

    for s in range(STAGES):
        z2[s].wait_recv()
        m2[s].start()
        if s + 1 < STAGES:
            z1[s + 1].wait_recv()
            z2[s + 1].start()
            m1[s + 1].start()
        m1_in[s].wait_recv()
        m2_in[s].wait_recv()
        for c in range(2):
            unit(s, c, 0)
        for copy in xq[s]:
            copy.wait_recv()
        for c in range(2):
            unit(s, c, 1)
        dq_far[s].start()
        dq_near[s].start()
        for piece in pieces:
            mate_out[s, piece[0]:piece[1]] = product(other, s, piece).astype(jnp.bfloat16)
        mt[s].start()
        for piece in pieces:
            mine[piece[0]:piece[1]] = product(core, s, piece)
        mt[s].wait_recv()
        r2_out[s] = (mine[0:TOK] + mate_in[s, 0:TOK].astype(jnp.float32)).astype(jnp.bfloat16)
        r2[s].start()
        hop1[s] = mine[TOK:REACH] + mate_in[s, TOK:REACH].astype(jnp.float32)
        hop0[s] = mine[REACH:WIN] + mate_in[s, REACH:WIN].astype(jnp.float32)
        if s > 0:
            middle(s - 1)
    finish(0)
    middle(1)
    finish(1)

    for s in range(STAGES):
        for copy in (z1[s], z2[s], m1[s], m2[s], *xq[s], mt[s], r2[s], r1[s], dq_far[s]):
            copy.wait_send()
        dq_far_in[s].wait_recv()
        dq_near[s].wait()
        for which, out in ((0, dk_ref), (1, dv_ref)):
            @pl.when(core == which)
            def _(out=out, away=(dv_ref if which == 0 else dk_ref)):
                block = pl.ds(0, 128)
                for step, device in enumerate((partner, diagonal, mate)):
                    remote(fin.at[s, block], out.at[:, cols(chip, s)],
                           f_s.at[s, step], f_r.at[s, step], device).wait_send()
                remote(fin.at[s, block], out.at[:, cols(1 - chip, s)],
                       f_s.at[s, 0], f_r.at[s, 0], partner).wait_recv()
                remote(fin.at[s, block], away.at[:, cols(1 - chip, s)],
                       f_s.at[s, 1], f_r.at[s, 1], diagonal).wait_recv()
                remote(fin.at[s, block], away.at[:, cols(chip, s)],
                       f_s.at[s, 2], f_r.at[s, 2], mate).wait_recv()
                pltpu.make_async_copy(fin.at[s, block], out.at[:, cols(chip, s)], f_l.at[s]).wait()


def local(ctx_size, queries, keys, values, grad_out, doc_lengths):
    bf16, f32 = jnp.bfloat16, jnp.float32
    anywhere = pl.BlockSpec(memory_space=pl.ANY)
    pair = pltpu.SemaphoreType.DMA((STAGES,))
    block16 = pltpu.VMEM((STAGES, TOK, HD), bf16)
    block32 = pltpu.VMEM((STAGES, TOK, HD), f32)
    dq, dk, dv = pl.pallas_call(
        lambda *refs: kernel(ctx_size, *refs),
        out_shape=(
            jax.ShapeDtypeStruct((2, HALF, KVH * HD), bf16),
            jax.ShapeDtypeStruct((128, KVH * HD), bf16),
            jax.ShapeDtypeStruct((128, KVH * HD), bf16),
        ),
        in_specs=[anywhere] * 4 + [pl.BlockSpec(memory_space=pltpu.VMEM)],
        out_specs=(anywhere,) * 3,
        scratch_shapes=[
            pltpu.VMEM((2, STAGES, WIN, HD), bf16),
            pltpu.VMEM((2, STAGES, 2, 2, HALF, HD), bf16),
            pltpu.VMEM((2, WIN, 2 * TOK), bf16),
            pltpu.VMEM((WIN, HD), f32),
            pltpu.VMEM((STAGES, 2, 2, HALF, HD), bf16),
            pltpu.VMEM((8, TOK), jnp.int32),
            pltpu.VMEM((STAGES, WIN, HD), bf16),
            pltpu.VMEM((STAGES, WIN, HD), bf16),
            block32, block32,
            block16, block16, block16, block16, block16,
            pltpu.SemaphoreType.DMA((4, STAGES)),
            pair, pair, pair, pair, pair, pair, pair, pair,
            pltpu.SemaphoreType.DMA((2, STAGES)), pltpu.SemaphoreType.DMA((2, STAGES)),
            pair, pair, pair, pair, pair, pair, pair, pair, pair,
            pltpu.SemaphoreType.DMA((STAGES, 3)), pltpu.SemaphoreType.DMA((STAGES, 3)), pair,
        ],
        compiler_params=pltpu.CompilerParams(
            collective_id=0, has_side_effects=True, vmem_limit_bytes=56 * 2**20),
        cost_estimate=pl.CostEstimate(
            flops=10 * 4 * TOK * SPAN * HD, bytes_accessed=4 * 2**20, transcendentals=4 * TOK * SPAN),
        name="attention_backward",
    )(queries.reshape(2, HALF, KVH * HD), keys, values, grad_out.reshape(2, HALF, KVH * HD),
      doc_lengths.reshape(1, 64))
    return dq.reshape(TOK, 1, KVH * HD), dk, dv


def solution(mesh):
    placed = (P("ctx", "head", None), P("ctx", None), P("ctx", None), P("ctx", "head", None), P())
    ctx_size = mesh.shape["ctx"]
    return jax.shard_map(
        lambda *args: local(ctx_size, *args),
        mesh=mesh,
        in_specs=placed,
        out_specs=(P("ctx", "head", None), P(("ctx", "head"), None), P(("ctx", "head"), None)),
        check_vma=False,
    )
```

```python
import math

import jax
import jax.numpy as jnp
from jax import lax
from jax.experimental import pallas as pl
from jax.experimental.pallas import tpu as pltpu
from jax.sharding import PartitionSpec as P

HD = 128
KVH = 4
TOK = 512
HALF = 256
REACH = 1024
WIN = REACH + TOK
SPAN = REACH + HALF
TILE = 64
STAGES = 2
MESH = pl.DeviceIdType.MESH
SCALE = 1.0 / math.sqrt(HD)
LOG2E = math.log2(math.e)
NT = (((1,), (1,)), ((), ()))
TN = (((0,), (0,)), ((), ()))


def mm(a, b):
    return jnp.dot(a, b, preferred_element_type=jnp.float32)


def kernel(
    ctx_size,
    q_ref, k_ref, v_ref, g_ref, len_ref,
    dq_ref, dk_ref, dv_ref,
    win, qo, pd, score, wgrad, mine, dqs, key_doc, query_doc,
    mate_out, mate_in, hop1, r2_out, r2_in, r1_out, r1_in, h0_out, h0_in,
    load_sem, z1_s, z1_r, z2_s, z2_r, m1_s, m1_r, m2_s, m2_r, x_s, x_r,
    mt_s, mt_r, r2_s, r2_r, r1_s, r1_r, dq_s, dq_r, dq_l, h0_s, h0_r,
):
    ctx = lax.axis_index("ctx")
    head = lax.axis_index("head")
    core = lax.rem(head, 2)
    chip = head // 2
    other = 1 - core
    nxt = (lax.rem(ctx + 1, ctx_size), head)
    prv = (lax.rem(ctx + ctx_size - 1, ctx_size), head)
    mate = (ctx, chip * 2 + other)
    partner = (ctx, (1 - chip) * 2 + core)
    diagonal = (ctx, (1 - chip) * 2 + other)
    stages, halves = range(STAGES), range(2)

    def cols(owner, s):
        return pl.ds(pl.multiple_of((owner * 2 + s) * HD, HD), HD)

    def remote(src, dst, send, recv, device):
        return pltpu.make_async_remote_copy(
            src_ref=src, dst_ref=dst, send_sem=send, recv_sem=recv,
            device_id=device, device_id_type=MESH,
        )

    own_rows = pl.ds(REACH, TOK)
    hop1_rows = pl.ds(TOK, TOK)
    hop2_rows = pl.ds(0, TOK)

    loads = []
    for s in stages:
        for kind, ref in ((0, k_ref), (1, v_ref)):
            loads.append(pltpu.make_async_copy(
                ref.at[:, cols(chip, s)], win.at[kind, s, own_rows], load_sem.at[kind, s]))
        for kind, ref in ((0, q_ref), (1, g_ref)):
            loads.append(pltpu.make_async_copy(
                ref.at[:, :, cols(chip, s)], qo.at[kind, s, :, 0], load_sem.at[2 + kind, s]))
    for load in loads:
        load.start()

    barrier = pltpu.get_barrier_semaphore()
    for device in (mate, partner, diagonal, *[(nxt[0], h) for h in range(4)], *[(prv[0], h) for h in range(4)]):
        pl.semaphore_signal(barrier, 1, device_id=device, device_id_type=MESH)

    for load in loads:
        load.wait()
    pl.semaphore_wait(barrier, 11)

    z1 = [remote(win.at[core, s, own_rows], win.at[core, s, hop1_rows], z1_s.at[s], z1_r.at[s], nxt) for s in stages]
    z2 = [remote(win.at[core, s, hop1_rows], win.at[core, s, hop2_rows], z2_s.at[s], z2_r.at[s], nxt) for s in stages]
    m1 = [remote(win.at[core, s, hop1_rows], win.at[core, s, hop1_rows], m1_s.at[s], m1_r.at[s], mate)
          for s in stages]
    m1_in = [remote(win.at[other, s, hop1_rows], win.at[other, s, hop1_rows], m1_s.at[s], m1_r.at[s], mate)
             for s in stages]
    m2 = [remote(win.at[core, s, hop2_rows], win.at[core, s, hop2_rows], m2_s.at[s], m2_r.at[s], mate)
          for s in stages]
    m2_in = [remote(win.at[other, s, hop2_rows], win.at[other, s, hop2_rows], m2_s.at[s], m2_r.at[s], mate)
             for s in stages]
    xq = [[remote(ref.at[:, :, cols(1 - chip, s)], qo.at[kind, s, :, 1], x_s.at[kind, s], x_r.at[kind, s], partner)
           for kind, ref in ((0, q_ref), (1, g_ref))] for s in stages]
    mate_rows = (hop2_rows, pl.ds(TOK, 2 * TOK))
    mt = [[remote(mate_out.at[s, mate_rows[h]], mate_in.at[s, mate_rows[h]], mt_s.at[s, h], mt_r.at[s, h], mate)
           for h in halves] for s in stages]
    quarters = [pl.ds(q * 128, 128) for q in range(4)]
    r2 = [[remote(r2_out.at[s, rows], r2_in.at[s, rows], r2_s.at[s, q], r2_r.at[s, q], prv)
           for q, rows in enumerate(quarters)] for s in stages]
    r1 = [[remote(r1_out.at[s, rows], r1_in.at[s, head], r1_s.at[s, q], r1_r.at[s, head], (prv[0], q))
           for q, rows in enumerate(quarters)] for s in stages]
    r1_from = [[remote(r1_out.at[s, quarters[0]], r1_in.at[s, h], r1_s.at[s, 0], r1_r.at[s, h], prv)
                for h in range(4)] for s in stages]
    h0 = [[remote(h0_out.at[s, rows], h0_in.at[s, head], h0_s.at[s, q], h0_r.at[s, head], (ctx, q))
           for q, rows in enumerate(quarters)] for s in stages]
    h0_from = [[remote(h0_out.at[s, quarters[0]], h0_in.at[s, h], h0_s.at[s, 0], h0_r.at[s, h], mate)
                for h in range(4)] for s in stages]
    dq_far = [remote(dqs.at[s, 1], dq_ref.at[:, :, cols(chip, s)], dq_s.at[s], dq_r.at[s], partner)
              for s in stages]
    dq_far_in = [remote(dqs.at[s, 1], dq_ref.at[:, :, cols(1 - chip, s)], dq_s.at[s], dq_r.at[s], partner)
                 for s in stages]
    dq_near = [pltpu.make_async_copy(dqs.at[s, 0], dq_ref.at[:, :, cols(chip, s)], dq_l.at[s])
               for s in stages]

    for copy in (*z1, *xq[0], *xq[1]):
        copy.start()

    lengths = len_ref[...]
    upto = jnp.where(
        lax.broadcasted_iota(jnp.int32, (64, HD), 0) <= lax.broadcasted_iota(jnp.int32, (64, HD), 1), 1.0, 0.0
    ).astype(jnp.bfloat16)

    def ends_of(part):
        rows = jnp.broadcast_to(part, (16, 64)).astype(jnp.float32).astype(jnp.bfloat16)
        return mm(rows, upto)[0:1]

    ends = (ends_of(lengths >> 5) * 32.0 + ends_of(lengths & 31)).astype(jnp.int32)
    wide = (16, 64)
    before = jnp.where(
        lax.broadcasted_iota(jnp.int32, (64, HD), 0) < lax.broadcasted_iota(jnp.int32, (64, HD), 1), 1.0, 0.0
    ).astype(jnp.bfloat16)

    def starts_of(part):
        rows = jnp.broadcast_to(part, wide).astype(jnp.float32).astype(jnp.bfloat16)
        return mm(rows, before)[0:1]

    starts = (starts_of(lengths >> 5) * 32.0 + starts_of(lengths & 31)).astype(jnp.int32)
    lane = lax.broadcasted_iota(jnp.int32, (1, HD), 1)
    starts = jnp.where(lane == 64, -WIN, starts)
    ends = jnp.where(lane == 64, 0, ends)

    def inside(count, base):
        pos = lax.broadcasted_iota(jnp.int32, (count, HD), 0) + base
        return (starts <= pos) & (pos < ends)

    for t in range(0, WIN, HALF):
        key_doc[t:t + HALF] = jnp.where(inside(HALF, ctx * TOK - REACH + t), 1.0, 0.0).astype(jnp.bfloat16)
    for t in range(0, TOK, HALF):
        query_doc[t:t + HALF] = jnp.where(inside(HALF, ctx * TOK + t), 0.0, -1e30).astype(jnp.bfloat16)

    causal = (lax.broadcasted_iota(jnp.int32, (HALF, HALF), 0)
              <= lax.broadcasted_iota(jnp.int32, (HALF, HALF), 1))

    def fold(x):
        return jnp.sum(x.reshape(x.shape[0] // 8, 8, x.shape[1]), axis=0)

    tiles = tuple(range(0, SPAN, TILE))

    def unit(s, c, j):
        low = c * HALF
        rows = pl.ds(low, SPAN)
        keyed = jnp.concatenate([win[0, s, rows], key_doc[rows]], axis=1)
        asked = jnp.concatenate([qo[0, s, c, j], query_doc[low:low + HALF]], axis=1)
        score[...] = lax.dot_general(keyed, asked, NT, preferred_element_type=jnp.float32)
        wgrad[...] = lax.dot_general(
            win[1, s, rows], qo[1, s, c, j], NT, preferred_element_type=jnp.float32)
        diagonal_rows = jnp.where(causal, score[REACH:SPAN], -1e30)
        score[REACH:SPAN] = diagonal_rows
        peak = None
        for t in tiles:
            x = score[t:t + TILE]
            x = jnp.max(x.reshape(TILE // 8, 8, HALF), axis=0)
            peak = x if peak is None else jnp.maximum(peak, x)
        top = jnp.max(peak, axis=0, keepdims=True)
        total = jnp.zeros((8, HALF), jnp.float32)
        dots = jnp.zeros((8, HALF), jnp.float32)
        for t in tiles:
            e = jnp.exp2((score[t:t + TILE] - top) * (SCALE * LOG2E))
            score[t:t + TILE] = e
            total += fold(e)
            dots += fold(e * wgrad[t:t + TILE])
        inverse = 1.0 / jnp.sum(total, axis=0, keepdims=True)
        delta = jnp.sum(dots, axis=0, keepdims=True) * inverse
        at = pl.ds(c * TOK + j * HALF, HALF)
        for t in tiles:
            weights = score[t:t + TILE] * inverse
            pd[s, 1, low + t:low + t + TILE, at] = weights.astype(jnp.bfloat16)
            pd[s, 0, low + t:low + t + TILE, at] = (weights * (wgrad[t:t + TILE] - delta)).astype(jnp.bfloat16)

    def query_grads(s):
        for c in halves:
            rows = pl.ds(c * HALF, SPAN)
            found = lax.dot_general(
                pd[s, 0, rows, c * TOK:(c + 1) * TOK], win[0, s, rows], TN, preferred_element_type=jnp.float32)
            dqs[s, :, c] = (found * SCALE).astype(jnp.bfloat16).reshape(2, HALF, HD)
        dq_far[s].start()
        dq_near[s].start()

    pieces = (((0, HALF, 0, 1), (HALF, TOK, 0, 2)), ((TOK, SPAN, 0, 2), (SPAN, WIN, 1, 2)))

    def product(kind, s, piece):
        low, high, c0, c1 = piece
        right = qo[kind, s, c0:c1].reshape(((c1 - c0) * TOK, HD))
        return mm(pd[s, kind, low:high, c0 * TOK:c1 * TOK], right) * jnp.where(kind == 0, SCALE, 1.0)

    def theirs(s, h):
        for piece in pieces[h]:
            mate_out[s, piece[0]:piece[1]] = product(other, s, piece).astype(jnp.bfloat16)
        mt[s][h].start()

    def ours(s, h):
        for piece in pieces[h]:
            mine[piece[0]:piece[1]] = product(core, s, piece)

    def outer(s):
        theirs(s, 0)
        ours(s, 0)
        theirs(s, 1)
        mt[s][0].wait_recv()
        for q in range(4):
            at = slice(q * 128, (q + 1) * 128)
            r2_out[s, at] = (mine[at] + mate_in[s, at].astype(jnp.float32)).astype(jnp.bfloat16)
            r2[s][q].start()
        ours(s, 1)
        mt[s][1].wait_recv()
        hop1[s] = mine[TOK:REACH] + mate_in[s, TOK:REACH].astype(jnp.float32)
        h0_out[s] = (mine[REACH:WIN] + mate_in[s, REACH:WIN].astype(jnp.float32)).astype(jnp.bfloat16)
        for q in range(4):
            @pl.when(head != q)
            def _(q=q):
                h0[s][q].start()

            @pl.when(head == q)
            def _(q=q):
                pltpu.make_async_copy(h0_out.at[s, quarters[q]], h0_in.at[s, q], h0_r.at[s, q]).start()

    def middle(s):
        for q in range(4):
            at = slice(q * 128, (q + 1) * 128)
            r2[s][q].wait_recv()
            r1_out[s, at] = (hop1[s, at] + r2_in[s, at].astype(jnp.float32)).astype(jnp.bfloat16)
            r1[s][q].start()

    def finish(s):
        for h in range(4):
            h0_from[s][h].wait_recv()
            r1_from[s][h].wait_recv()
            out = (dk_ref, dv_ref)[h % 2]
            g = (h // 2) * 2 + s
            out[:, g * HD:(g + 1) * HD] = (
                h0_in[s, h].astype(jnp.float32) + r1_in[s, h].astype(jnp.float32)).astype(jnp.bfloat16)

    def forward(s):
        z1[s].wait_recv()
        z2[s].start()
        m1[s].start()

    def arrive(s):
        z2[s].wait_recv()
        m2[s].start()

    forward(0)
    forward(1)
    arrive(0)
    m1_in[0].wait_recv()
    m2_in[0].wait_recv()
    unit(0, 0, 0)
    unit(0, 1, 0)
    for copy in xq[0]:
        copy.wait_recv()
    unit(0, 0, 1)
    arrive(1)
    unit(0, 1, 1)
    outer(0)
    m1_in[1].wait_recv()
    m2_in[1].wait_recv()
    unit(1, 0, 0)
    unit(1, 1, 0)
    middle(0)
    for copy in xq[1]:
        copy.wait_recv()
    unit(1, 0, 1)
    unit(1, 1, 1)
    outer(1)
    query_grads(1)
    query_grads(0)
    middle(1)
    finish(0)
    finish(1)

    for s in stages:
        for copy in (z1[s], z2[s], m1[s], m2[s], *xq[s], *mt[s], *r2[s], *r1[s], dq_far[s]):
            copy.wait_send()
        for q in range(4):
            @pl.when(head != q)
            def _(q=q):
                h0[s][q].wait_send()
        dq_far_in[s].wait_recv()
        dq_near[s].wait()


def local(ctx_size, queries, keys, values, grad_out, doc_lengths):
    bf16, f32 = jnp.bfloat16, jnp.float32
    anywhere = pl.BlockSpec(memory_space=pl.ANY)
    pair = pltpu.SemaphoreType.DMA((STAGES,))
    quad = pltpu.SemaphoreType.DMA((STAGES, 2))
    eight = pltpu.SemaphoreType.DMA((STAGES, 4))
    block16 = pltpu.VMEM((STAGES, TOK, HD), bf16)
    heads16 = pltpu.VMEM((STAGES, 4, 128, HD), bf16)
    dq, dk, dv = pl.pallas_call(
        lambda *refs: kernel(ctx_size, *refs),
        out_shape=(
            pltpu.VMEM((2, HALF, KVH * HD), bf16),
            pltpu.VMEM((128, KVH * HD), bf16),
            pltpu.VMEM((128, KVH * HD), bf16),
        ),
        in_specs=[anywhere] * 4 + [pl.BlockSpec(memory_space=pltpu.VMEM)],
        out_specs=(pl.BlockSpec(memory_space=pltpu.VMEM), pl.BlockSpec(memory_space=pltpu.VMEM), pl.BlockSpec(memory_space=pltpu.VMEM)),
        scratch_shapes=[
            pltpu.VMEM((2, STAGES, WIN, HD), bf16),
            pltpu.VMEM((2, STAGES, 2, 2, HALF, HD), bf16),
            pltpu.VMEM((STAGES, 2, WIN, 2 * TOK), bf16),
            pltpu.VMEM((SPAN, HALF), f32),
            pltpu.VMEM((SPAN, HALF), f32),
            pltpu.VMEM((WIN, HD), f32),
            pltpu.VMEM((STAGES, 2, 2, HALF, HD), bf16),
            pltpu.VMEM((WIN, HD), bf16),
            pltpu.VMEM((TOK, HD), bf16),
            pltpu.VMEM((STAGES, WIN, HD), bf16),
            pltpu.VMEM((STAGES, WIN, HD), bf16),
            pltpu.VMEM((STAGES, TOK, HD), f32),
            block16, block16, block16, heads16, block16, heads16,
            pltpu.SemaphoreType.DMA((4, STAGES)),
            pair, pair, pair, pair, pair, pair, pair, pair,
            quad, quad,
            quad, quad, eight, eight, eight, eight, pair, pair, pair,
            eight, eight,
        ],
        compiler_params=pltpu.CompilerParams(
            collective_id=0, has_side_effects=True, vmem_limit_bytes=56 * 2**20),
        cost_estimate=pl.CostEstimate(
            flops=10 * 4 * TOK * SPAN * HD, bytes_accessed=4 * 2**20, transcendentals=4 * TOK * SPAN),
        name="attention_backward",
    )(queries.reshape(2, HALF, KVH * HD), keys, values, grad_out.reshape(2, HALF, KVH * HD),
      doc_lengths.reshape(1, 64))
    return dq.reshape(TOK, 1, KVH * HD), dk, dv


def solution(mesh):
    placed = (P("ctx", "head", None), P("ctx", None), P("ctx", None), P("ctx", "head", None), P())
    ctx_size = mesh.shape["ctx"]
    return jax.shard_map(
        lambda *args: local(ctx_size, *args),
        mesh=mesh,
        in_specs=placed,
        out_specs=(P("ctx", "head", None), P(("ctx", "head"), None), P(("ctx", "head"), None)),
        check_vma=False,
    )
```

```python
import math

import jax
import jax.numpy as jnp
from jax import lax
from jax.experimental import pallas as pl
from jax.experimental.pallas import tpu as pltpu
from jax.sharding import PartitionSpec as P

HD = 128
KVH = 4
TOK = 512
HALF = 256
REACH = 1024
WIN = REACH + TOK
SPAN = REACH + HALF
TILE = 64
STAGES = 2
ROW = 8
MESH = pl.DeviceIdType.MESH
SCALE = 1.0 / math.sqrt(HD)
LOG2E = math.log2(math.e)
NT = (((1,), (1,)), ((), ()))
TN = (((0,), (0,)), ((), ()))


def mm(a, b):
    return jnp.dot(a, b, preferred_element_type=jnp.float32)


def kernel(
    ctx_size,
    q_ref, k_ref, v_ref, g_ref, len_ref,
    dq_ref, dk_ref, dv_ref,
    win, qo, pd, score_a, score_b, wgrad_a, wgrad_b, mine, dqs, key_doc, query_doc,
    mate_out, mate_in, hop1, r2_out, r2_in, r1_out, r1_in, h0_out, h0_in, relay,
    load_sem, z1_s, z1_r, z2_s, z2_r, m1_s, m1_r, m2_s, m2_r, x_s, x_r,
    mt_s, mt_r, r2_s, r2_r, r1_s, r1_r, dq_s, dq_r, dq_l, h0_s, h0_r, relay_s, relay_r,
):
    ctx = lax.axis_index("ctx")
    head = lax.axis_index("head")
    core = lax.rem(head, 2)
    chip = head // 2
    other = 1 - core
    nxt = (lax.rem(ctx + 1, ctx_size), head)
    prv = (lax.rem(ctx + ctx_size - 1, ctx_size), head)
    mate = (ctx, chip * 2 + other)
    partner = (ctx, (1 - chip) * 2 + core)
    diagonal = (ctx, (1 - chip) * 2 + other)
    stages, halves = range(STAGES), range(2)
    place = lax.rem(ctx, ROW)
    at_start, at_end = place == 0, place == ROW - 1

    def near(steps):
        return (lax.rem(ctx + ctx_size + steps, ctx_size), head)

    relay_to, relay_from, relay_down, relay_up = near(ROW), near(-ROW), near(1 - ROW), near(ROW - 1)

    def cols(owner, s):
        return pl.ds(pl.multiple_of((owner * 2 + s) * HD, HD), HD)

    def remote(src, dst, send, recv, device):
        return pltpu.make_async_remote_copy(
            src_ref=src, dst_ref=dst, send_sem=send, recv_sem=recv,
            device_id=device, device_id_type=MESH,
        )

    own_rows = pl.ds(REACH, TOK)
    hop1_rows = pl.ds(TOK, TOK)
    hop2_rows = pl.ds(0, TOK)

    loads = []
    for s in stages:
        for kind, ref in ((0, k_ref), (1, v_ref)):
            loads.append(pltpu.make_async_copy(
                ref.at[:, cols(chip, s)], win.at[kind, s, own_rows], load_sem.at[kind, s]))
        for kind, ref in ((0, q_ref), (1, g_ref)):
            loads.append(pltpu.make_async_copy(
                ref.at[:, :, cols(chip, s)], qo.at[kind, s, :, 0], load_sem.at[2 + kind, s]))
    for load in loads:
        load.start()

    barrier = pltpu.get_barrier_semaphore()
    for device in (mate, partner, diagonal, *[(nxt[0], h) for h in range(4)], *[(prv[0], h) for h in range(4)]):
        pl.semaphore_signal(barrier, 1, device_id=device, device_id_type=MESH)

    @pl.when(at_end)
    def _():
        for device in (relay_to, relay_from, relay_down):
            pl.semaphore_signal(barrier, 1, device_id=device, device_id_type=MESH)

    @pl.when(at_start)
    def _():
        pl.semaphore_signal(barrier, 1, device_id=relay_up, device_id_type=MESH)

    for load in loads:
        load.wait()
    pl.semaphore_wait(barrier, 11 + 3 * (place // (ROW - 1)) + (ROW - 1 - place) // (ROW - 1))

    z1 = [remote(win.at[core, s, own_rows], win.at[core, s, hop1_rows], z1_s.at[s], z1_r.at[s], nxt) for s in stages]
    z2 = [remote(win.at[core, s, hop1_rows], win.at[core, s, hop2_rows], z2_s.at[s], z2_r.at[s], nxt) for s in stages]
    z1_relayed = remote(win.at[core, 1, own_rows], relay.at[0], z1_s.at[1], relay_r.at[0], relay_to)
    z2_relayed = remote(win.at[core, 1, hop1_rows], relay.at[1], z2_s.at[1], relay_r.at[1], relay_to)
    passed = [remote(relay.at[k], win.at[core, 1, rows], relay_s.at[k], sem.at[1], relay_down)
              for k, (rows, sem) in enumerate(((hop1_rows, z1_r), (hop2_rows, z2_r)))]
    m1 = [remote(win.at[core, s, hop1_rows], win.at[core, s, hop1_rows], m1_s.at[s], m1_r.at[s], mate)
          for s in stages]
    m1_in = [remote(win.at[other, s, hop1_rows], win.at[other, s, hop1_rows], m1_s.at[s], m1_r.at[s], mate)
             for s in stages]
    m2 = [remote(win.at[core, s, hop2_rows], win.at[core, s, hop2_rows], m2_s.at[s], m2_r.at[s], mate)
          for s in stages]
    m2_in = [remote(win.at[other, s, hop2_rows], win.at[other, s, hop2_rows], m2_s.at[s], m2_r.at[s], mate)
             for s in stages]
    xq = [[remote(ref.at[:, :, cols(1 - chip, s)], qo.at[kind, s, :, 1], x_s.at[kind, s], x_r.at[kind, s], partner)
           for kind, ref in ((0, q_ref), (1, g_ref))] for s in stages]
    mate_rows = (hop2_rows, pl.ds(TOK, 2 * TOK))
    mt = [[remote(mate_out.at[s, mate_rows[h]], mate_in.at[s, mate_rows[h]], mt_s.at[s, h], mt_r.at[s, h], mate)
           for h in halves] for s in stages]
    quarters = [pl.ds(q * 128, 128) for q in range(4)]
    r2 = [[remote(r2_out.at[s, rows], r2_in.at[s, rows], r2_s.at[s, q], r2_r.at[s, q], prv)
           for q, rows in enumerate(quarters)] for s in stages]
    r1 = [[remote(r1_out.at[s, rows], r1_in.at[s, head], r1_s.at[s, q], r1_r.at[s, head], (prv[0], q))
           for q, rows in enumerate(quarters)] for s in stages]
    r1_from = [[remote(r1_out.at[s, quarters[0]], r1_in.at[s, h], r1_s.at[s, 0], r1_r.at[s, h], prv)
                for h in range(4)] for s in stages]
    h0 = [[remote(h0_out.at[s, rows], h0_in.at[s, head], h0_s.at[s, q], h0_r.at[s, head], (ctx, q))
           for q, rows in enumerate(quarters)] for s in stages]
    h0_from = [[remote(h0_out.at[s, quarters[0]], h0_in.at[s, h], h0_s.at[s, 0], h0_r.at[s, h], mate)
                for h in range(4)] for s in stages]
    dq_far = [remote(dqs.at[s, 1], dq_ref.at[:, :, cols(chip, s)], dq_s.at[s], dq_r.at[s], partner)
              for s in stages]
    dq_far_in = [remote(dqs.at[s, 1], dq_ref.at[:, :, cols(1 - chip, s)], dq_s.at[s], dq_r.at[s], partner)
                 for s in stages]
    dq_near = [pltpu.make_async_copy(dqs.at[s, 0], dq_ref.at[:, :, cols(chip, s)], dq_l.at[s])
               for s in stages]

    z1[0].start()

    def either(direct, relayed):
        @pl.when(at_end)
        def _():
            relayed.start()

        @pl.when(jnp.logical_not(at_end))
        def _():
            direct.start()

    either(z1[1], z1_relayed)
    for copy in (*xq[0], *xq[1]):
        copy.start()

    lengths = len_ref[...]
    upto = jnp.where(
        lax.broadcasted_iota(jnp.int32, (64, HD), 0) <= lax.broadcasted_iota(jnp.int32, (64, HD), 1), 1.0, 0.0
    ).astype(jnp.bfloat16)

    def ends_of(part):
        rows = jnp.broadcast_to(part, (16, 64)).astype(jnp.float32).astype(jnp.bfloat16)
        return mm(rows, upto)[0:1]

    ends = (ends_of(lengths >> 5) * 32.0 + ends_of(lengths & 31)).astype(jnp.int32)
    wide = (16, 64)
    before = jnp.where(
        lax.broadcasted_iota(jnp.int32, (64, HD), 0) < lax.broadcasted_iota(jnp.int32, (64, HD), 1), 1.0, 0.0
    ).astype(jnp.bfloat16)

    def starts_of(part):
        rows = jnp.broadcast_to(part, wide).astype(jnp.float32).astype(jnp.bfloat16)
        return mm(rows, before)[0:1]

    starts = (starts_of(lengths >> 5) * 32.0 + starts_of(lengths & 31)).astype(jnp.int32)
    lane = lax.broadcasted_iota(jnp.int32, (1, HD), 1)
    starts = jnp.where(lane == 64, -WIN, starts)
    ends = jnp.where(lane == 64, 0, ends)

    def inside(count, base):
        pos = lax.broadcasted_iota(jnp.int32, (count, HD), 0) + base
        return (starts <= pos) & (pos < ends)

    for t in range(0, WIN, HALF):
        key_doc[t:t + HALF] = jnp.where(inside(HALF, ctx * TOK - REACH + t), 1.0, 0.0).astype(jnp.bfloat16)
    for t in range(0, TOK, HALF):
        query_doc[t:t + HALF] = jnp.where(inside(HALF, ctx * TOK + t), 0.0, -1e30).astype(jnp.bfloat16)

    causal = (lax.broadcasted_iota(jnp.int32, (HALF, HALF), 0)
              <= lax.broadcasted_iota(jnp.int32, (HALF, HALF), 1))

    def fold(x):
        return jnp.sum(x.reshape(x.shape[0] // 8, 8, x.shape[1]), axis=0)

    scores, wgrads = (score_a, score_b), (wgrad_a, wgrad_b)
    tiles = tuple(range(0, SPAN, TILE))

    def open_unit(s, c, j, slot):
        low = c * HALF
        rows = pl.ds(low, SPAN)
        score, wgrad = scores[slot], wgrads[slot]
        keyed = jnp.concatenate([win[0, s, rows], key_doc[rows]], axis=1)
        asked = jnp.concatenate([qo[0, s, c, j], query_doc[low:low + HALF]], axis=1)
        score[...] = lax.dot_general(keyed, asked, NT, preferred_element_type=jnp.float32)
        wgrad[...] = lax.dot_general(
            win[1, s, rows], qo[1, s, c, j], NT, preferred_element_type=jnp.float32)

    def close_unit(s, c, j, slot):
        low = c * HALF
        score, wgrad = scores[slot], wgrads[slot]
        score[REACH:SPAN] = jnp.where(causal, score[REACH:SPAN], -1e30)
        peak = None
        for t in tiles:
            x = score[t:t + TILE]
            x = jnp.max(x.reshape(TILE // 8, 8, HALF), axis=0)
            peak = x if peak is None else jnp.maximum(peak, x)
        top = jnp.max(peak, axis=0, keepdims=True)
        total = jnp.zeros((8, HALF), jnp.float32)
        dots = jnp.zeros((8, HALF), jnp.float32)
        for t in tiles:
            e = jnp.exp2((score[t:t + TILE] - top) * (SCALE * LOG2E))
            score[t:t + TILE] = e
            total += fold(e)
            dots += fold(e * wgrad[t:t + TILE])
        inverse = 1.0 / jnp.sum(total, axis=0, keepdims=True)
        delta = jnp.sum(dots, axis=0, keepdims=True) * inverse
        at = pl.ds(c * TOK + j * HALF, HALF)
        for t in tiles:
            weights = score[t:t + TILE] * inverse
            pd[s, 1, low + t:low + t + TILE, at] = weights.astype(jnp.bfloat16)
            pd[s, 0, low + t:low + t + TILE, at] = (weights * (wgrad[t:t + TILE] - delta)).astype(jnp.bfloat16)

    def query_grads(s):
        for c in halves:
            rows = pl.ds(c * HALF, SPAN)
            found = lax.dot_general(
                pd[s, 0, rows, c * TOK:(c + 1) * TOK], win[0, s, rows], TN, preferred_element_type=jnp.float32)
            dqs[s, :, c] = (found * SCALE).astype(jnp.bfloat16).reshape(2, HALF, HD)
        dq_far[s].start()
        dq_near[s].start()

    pieces = (((0, HALF, 0, 1), (HALF, TOK, 0, 2)), ((TOK, SPAN, 0, 2), (SPAN, WIN, 1, 2)))

    def product(kind, s, piece):
        low, high, c0, c1 = piece
        right = qo[kind, s, c0:c1].reshape(((c1 - c0) * TOK, HD))
        return mm(pd[s, kind, low:high, c0 * TOK:c1 * TOK], right) * jnp.where(kind == 0, SCALE, 1.0)

    def theirs(s, h):
        for piece in pieces[h]:
            mate_out[s, piece[0]:piece[1]] = product(other, s, piece).astype(jnp.bfloat16)
        mt[s][h].start()

    def ours(s, h):
        for piece in pieces[h]:
            mine[piece[0]:piece[1]] = product(core, s, piece)

    def outer(s):
        theirs(s, 0)
        ours(s, 0)
        theirs(s, 1)
        mt[s][0].wait_recv()
        for q in range(4):
            at = slice(q * 128, (q + 1) * 128)
            r2_out[s, at] = (mine[at] + mate_in[s, at].astype(jnp.float32)).astype(jnp.bfloat16)
            r2[s][q].start()
        ours(s, 1)
        mt[s][1].wait_recv()
        hop1[s] = mine[TOK:REACH] + mate_in[s, TOK:REACH].astype(jnp.float32)
        h0_out[s] = (mine[REACH:WIN] + mate_in[s, REACH:WIN].astype(jnp.float32)).astype(jnp.bfloat16)
        for q in range(4):
            @pl.when(head != q)
            def _(q=q):
                h0[s][q].start()

            @pl.when(head == q)
            def _(q=q):
                pltpu.make_async_copy(h0_out.at[s, quarters[q]], h0_in.at[s, q], h0_r.at[s, q]).start()

    def middle(s):
        for q in range(4):
            at = slice(q * 128, (q + 1) * 128)
            r2[s][q].wait_recv()
            r1_out[s, at] = (hop1[s, at] + r2_in[s, at].astype(jnp.float32)).astype(jnp.bfloat16)
            r1[s][q].start()

    def finish(s):
        for h in range(4):
            h0_from[s][h].wait_recv()
            r1_from[s][h].wait_recv()
            out = (dk_ref, dv_ref)[h % 2]
            g = (h // 2) * 2 + s
            out[:, g * HD:(g + 1) * HD] = (
                h0_in[s, h].astype(jnp.float32) + r1_in[s, h].astype(jnp.float32)).astype(jnp.bfloat16)

    def forward(s):
        z1[s].wait_recv()
        if s == 1:
            either(z2[1], z2_relayed)
        else:
            z2[s].start()
        m1[s].start()

    def pass_on(k):
        @pl.when(at_end)
        def _():
            (z1_relayed, z2_relayed)[k].wait_recv()
            passed[k].start()

    def arrive(s):
        z2[s].wait_recv()
        m2[s].start()

    forward(0)

    @pl.when(jnp.logical_not(at_start))
    def _():
        forward(1)

    pass_on(0)
    arrive(0)
    m1_in[0].wait_recv()
    m2_in[0].wait_recv()
    open_unit(0, 0, 0, 0)
    open_unit(0, 1, 0, 1)
    close_unit(0, 0, 0, 0)

    @pl.when(at_start)
    def _():
        forward(1)

    for copy in xq[0]:
        copy.wait_recv()
    open_unit(0, 0, 1, 0)
    close_unit(0, 1, 0, 1)
    pass_on(1)
    open_unit(0, 1, 1, 1)
    close_unit(0, 0, 1, 0)
    close_unit(0, 1, 1, 1)
    outer(0)
    arrive(1)
    query_grads(0)
    m1_in[1].wait_recv()
    m2_in[1].wait_recv()
    open_unit(1, 0, 0, 0)
    open_unit(1, 1, 0, 1)
    close_unit(1, 0, 0, 0)
    for copy in xq[1]:
        copy.wait_recv()
    open_unit(1, 0, 1, 0)
    close_unit(1, 1, 0, 1)
    middle(0)
    open_unit(1, 1, 1, 1)
    close_unit(1, 0, 1, 0)
    close_unit(1, 1, 1, 1)
    outer(1)
    query_grads(1)
    middle(1)
    finish(0)
    finish(1)

    @pl.when(at_end)
    def _():
        for copy in passed:
            copy.wait_send()

    for s in stages:
        for copy in (z1[s], z2[s], m1[s], m2[s], *xq[s], *mt[s], *r2[s], *r1[s], dq_far[s]):
            copy.wait_send()
        for q in range(4):
            @pl.when(head != q)
            def _(q=q):
                h0[s][q].wait_send()
        dq_far_in[s].wait_recv()
        dq_near[s].wait()


def local(ctx_size, queries, keys, values, grad_out, doc_lengths):
    bf16, f32 = jnp.bfloat16, jnp.float32
    anywhere = pl.BlockSpec(memory_space=pl.ANY)
    pair = pltpu.SemaphoreType.DMA((STAGES,))
    quad = pltpu.SemaphoreType.DMA((STAGES, 2))
    eight = pltpu.SemaphoreType.DMA((STAGES, 4))
    block16 = pltpu.VMEM((STAGES, TOK, HD), bf16)
    unit32 = pltpu.VMEM((SPAN, HALF), f32)
    heads16 = pltpu.VMEM((STAGES, 4, 128, HD), bf16)
    dq, dk, dv = pl.pallas_call(
        lambda *refs: kernel(ctx_size, *refs),
        out_shape=(
            pltpu.VMEM((2, HALF, KVH * HD), bf16),
            pltpu.VMEM((128, KVH * HD), bf16),
            pltpu.VMEM((128, KVH * HD), bf16),
        ),
        in_specs=[anywhere] * 4 + [pl.BlockSpec(memory_space=pltpu.VMEM)],
        out_specs=(pl.BlockSpec(memory_space=pltpu.VMEM), pl.BlockSpec(memory_space=pltpu.VMEM), pl.BlockSpec(memory_space=pltpu.VMEM)),
        scratch_shapes=[
            pltpu.VMEM((2, STAGES, WIN, HD), bf16),
            pltpu.VMEM((2, STAGES, 2, 2, HALF, HD), bf16),
            pltpu.VMEM((STAGES, 2, WIN, 2 * TOK), bf16),
            unit32, unit32, unit32, unit32,
            pltpu.VMEM((WIN, HD), f32),
            pltpu.VMEM((STAGES, 2, 2, HALF, HD), bf16),
            pltpu.VMEM((WIN, HD), bf16),
            pltpu.VMEM((TOK, HD), bf16),
            pltpu.VMEM((STAGES, WIN, HD), bf16),
            pltpu.VMEM((STAGES, WIN, HD), bf16),
            pltpu.VMEM((STAGES, TOK, HD), f32),
            block16, block16, block16, heads16, block16, heads16,
            block16,
            pltpu.SemaphoreType.DMA((4, STAGES)),
            pair, pair, pair, pair, pair, pair, pair, pair,
            quad, quad,
            quad, quad, eight, eight, eight, eight, pair, pair, pair,
            eight, eight,
            pair, pair,
        ],
        compiler_params=pltpu.CompilerParams(
            collective_id=0, has_side_effects=True, vmem_limit_bytes=56 * 2**20),
        cost_estimate=pl.CostEstimate(
            flops=10 * 4 * TOK * SPAN * HD, bytes_accessed=4 * 2**20, transcendentals=4 * TOK * SPAN),
        name="attention_backward",
    )(queries.reshape(2, HALF, KVH * HD), keys, values, grad_out.reshape(2, HALF, KVH * HD),
      doc_lengths.reshape(1, 64))
    return dq.reshape(TOK, 1, KVH * HD), dk, dv


def solution(mesh):
    placed = (P("ctx", "head", None), P("ctx", None), P("ctx", None), P("ctx", "head", None), P())
    ctx_size = mesh.shape["ctx"]
    return jax.shard_map(
        lambda *args: local(ctx_size, *args),
        mesh=mesh,
        in_specs=placed,
        out_specs=(P("ctx", "head", None), P(("ctx", "head"), None), P(("ctx", "head"), None)),
        check_vma=False,
    )
```

```python
import math

import jax
import jax.numpy as jnp
from jax import lax
from jax.experimental import pallas as pl
from jax.experimental.pallas import tpu as pltpu
from jax.sharding import PartitionSpec as P

HD = 128
KVH = 4
TOK = 512
HALF = 256
REACH = 1024
WIN = REACH + TOK
SPAN = REACH + HALF
TILE = 64
STAGES = 2
ROW = 8
MESH = pl.DeviceIdType.MESH
SCALE = 1.0 / math.sqrt(HD)
LOG2E = math.log2(math.e)
NT = (((1,), (1,)), ((), ()))
TN = (((0,), (0,)), ((), ()))


def mm(a, b):
    return jnp.dot(a, b, preferred_element_type=jnp.float32)


def kernel(
    ctx_size,
    q_ref, k_ref, v_ref, g_ref, len_ref,
    dq_ref, dk_ref, dv_ref,
    win, qo, pd, scores, wgrads, stats, mine, dqs, key_doc, query_doc,
    mate_out, mate_in, hop1, r2_out, r2_in, r1_out, r1_in, h0_out, h0_in, relay,
    load_sem, z1_s, z1_r, z2_s, z2_r, m1_s, m1_r, m2_s, m2_r, x_s, x_r,
    mt_s, mt_r, r2_s, r2_r, r1_s, r1_r, dq_s, dq_r, dq_l, h0_s, h0_r, relay_s, relay_r,
):
    ctx = lax.axis_index("ctx")
    head = lax.axis_index("head")
    core = lax.rem(head, 2)
    chip = head // 2
    other = 1 - core
    nxt = (lax.rem(ctx + 1, ctx_size), head)
    prv = (lax.rem(ctx + ctx_size - 1, ctx_size), head)
    mate = (ctx, chip * 2 + other)
    partner = (ctx, (1 - chip) * 2 + core)
    diagonal = (ctx, (1 - chip) * 2 + other)
    stages, halves = range(STAGES), range(2)
    place = lax.rem(ctx, ROW)
    at_start, at_end = place == 0, place == ROW - 1

    def near(steps):
        return (lax.rem(ctx + ctx_size + steps, ctx_size), head)

    relay_to, relay_from, relay_down, relay_up = near(ROW), near(-ROW), near(1 - ROW), near(ROW - 1)

    def cols(owner, s):
        return pl.ds(pl.multiple_of((owner * 2 + s) * HD, HD), HD)

    def remote(src, dst, send, recv, device):
        return pltpu.make_async_remote_copy(
            src_ref=src, dst_ref=dst, send_sem=send, recv_sem=recv,
            device_id=device, device_id_type=MESH,
        )

    own_rows = pl.ds(REACH, TOK)
    hop1_rows = pl.ds(TOK, TOK)
    hop2_rows = pl.ds(0, TOK)

    loads = []
    for s in stages:
        for kind, ref in ((0, k_ref), (1, v_ref)):
            loads.append(pltpu.make_async_copy(
                ref.at[:, cols(chip, s)], win.at[kind, s, own_rows], load_sem.at[kind, s]))
        for kind, ref in ((0, q_ref), (1, g_ref)):
            loads.append(pltpu.make_async_copy(
                ref.at[:, :, cols(chip, s)], qo.at[kind, s, :, 0], load_sem.at[2 + kind, s]))
    for load in loads:
        load.start()

    barrier = pltpu.get_barrier_semaphore()
    for device in (mate, partner, diagonal, *[(nxt[0], h) for h in range(4)], *[(prv[0], h) for h in range(4)]):
        pl.semaphore_signal(barrier, 1, device_id=device, device_id_type=MESH)

    @pl.when(at_end)
    def _():
        for device in (relay_to, relay_from, relay_down):
            pl.semaphore_signal(barrier, 1, device_id=device, device_id_type=MESH)

    @pl.when(at_start)
    def _():
        pl.semaphore_signal(barrier, 1, device_id=relay_up, device_id_type=MESH)

    for load in loads:
        load.wait()
    pl.semaphore_wait(barrier, 11 + 3 * (place // (ROW - 1)) + (ROW - 1 - place) // (ROW - 1))

    z1 = [remote(win.at[core, s, own_rows], win.at[core, s, hop1_rows], z1_s.at[s], z1_r.at[s], nxt) for s in stages]
    z2 = [remote(win.at[core, s, hop1_rows], win.at[core, s, hop2_rows], z2_s.at[s], z2_r.at[s], nxt) for s in stages]
    z1_relayed = remote(win.at[core, 1, own_rows], relay.at[0], z1_s.at[1], relay_r.at[0], relay_to)
    z2_relayed = remote(win.at[core, 1, hop1_rows], relay.at[1], z2_s.at[1], relay_r.at[1], relay_to)
    passed = [remote(relay.at[k], win.at[core, 1, rows], relay_s.at[k], sem.at[1], relay_down)
              for k, (rows, sem) in enumerate(((hop1_rows, z1_r), (hop2_rows, z2_r)))]
    m1 = [remote(win.at[core, s, hop1_rows], win.at[core, s, hop1_rows], m1_s.at[s], m1_r.at[s], mate)
          for s in stages]
    m1_in = [remote(win.at[other, s, hop1_rows], win.at[other, s, hop1_rows], m1_s.at[s], m1_r.at[s], mate)
             for s in stages]
    m2 = [remote(win.at[core, s, hop2_rows], win.at[core, s, hop2_rows], m2_s.at[s], m2_r.at[s], mate)
          for s in stages]
    m2_in = [remote(win.at[other, s, hop2_rows], win.at[other, s, hop2_rows], m2_s.at[s], m2_r.at[s], mate)
             for s in stages]
    xq = [[remote(ref.at[:, :, cols(1 - chip, s)], qo.at[kind, s, :, 1], x_s.at[kind, s], x_r.at[kind, s], partner)
           for kind, ref in ((0, q_ref), (1, g_ref))] for s in stages]
    mate_rows = (hop2_rows, pl.ds(TOK, 2 * TOK))
    mt = [[remote(mate_out.at[s, mate_rows[h]], mate_in.at[s, mate_rows[h]], mt_s.at[s, h], mt_r.at[s, h], mate)
           for h in halves] for s in stages]
    quarters = [pl.ds(q * 128, 128) for q in range(4)]
    r2 = [[remote(r2_out.at[s, rows], r2_in.at[s, rows], r2_s.at[s, q], r2_r.at[s, q], prv)
           for q, rows in enumerate(quarters)] for s in stages]
    r1 = [[remote(r1_out.at[s, rows], r1_in.at[s, head], r1_s.at[s, q], r1_r.at[s, head], (prv[0], q))
           for q, rows in enumerate(quarters)] for s in stages]
    r1_from = [[remote(r1_out.at[s, quarters[0]], r1_in.at[s, h], r1_s.at[s, 0], r1_r.at[s, h], prv)
                for h in range(4)] for s in stages]
    h0 = [[remote(h0_out.at[s, rows], h0_in.at[s, head], h0_s.at[s, q], h0_r.at[s, head], (ctx, q))
           for q, rows in enumerate(quarters)] for s in stages]
    h0_from = [[remote(h0_out.at[s, quarters[0]], h0_in.at[s, h], h0_s.at[s, 0], h0_r.at[s, h], mate)
                for h in range(4)] for s in stages]
    dq_far = [remote(dqs.at[s, 1], dq_ref.at[:, :, cols(chip, s)], dq_s.at[s], dq_r.at[s], partner)
              for s in stages]
    dq_far_in = [remote(dqs.at[s, 1], dq_ref.at[:, :, cols(1 - chip, s)], dq_s.at[s], dq_r.at[s], partner)
                 for s in stages]
    dq_near = [pltpu.make_async_copy(dqs.at[s, 0], dq_ref.at[:, :, cols(chip, s)], dq_l.at[s])
               for s in stages]

    z1[0].start()

    def either(direct, relayed):
        @pl.when(at_end)
        def _():
            relayed.start()

        @pl.when(jnp.logical_not(at_end))
        def _():
            direct.start()

    either(z1[1], z1_relayed)
    for copy in (*xq[0], *xq[1]):
        copy.start()

    lengths = len_ref[...]
    upto = jnp.where(
        lax.broadcasted_iota(jnp.int32, (64, HD), 0) <= lax.broadcasted_iota(jnp.int32, (64, HD), 1), 1.0, 0.0
    ).astype(jnp.bfloat16)

    def ends_of(part):
        rows = jnp.broadcast_to(part, (16, 64)).astype(jnp.float32).astype(jnp.bfloat16)
        return mm(rows, upto)[0:1]

    ends = (ends_of(lengths >> 5) * 32.0 + ends_of(lengths & 31)).astype(jnp.int32)
    wide = (16, 64)
    before = jnp.where(
        lax.broadcasted_iota(jnp.int32, (64, HD), 0) < lax.broadcasted_iota(jnp.int32, (64, HD), 1), 1.0, 0.0
    ).astype(jnp.bfloat16)

    def starts_of(part):
        rows = jnp.broadcast_to(part, wide).astype(jnp.float32).astype(jnp.bfloat16)
        return mm(rows, before)[0:1]

    starts = (starts_of(lengths >> 5) * 32.0 + starts_of(lengths & 31)).astype(jnp.int32)
    lane = lax.broadcasted_iota(jnp.int32, (1, HD), 1)
    starts = jnp.where(lane == 64, -WIN, starts)
    ends = jnp.where(lane == 64, 0, ends)

    def inside(count, base):
        pos = lax.broadcasted_iota(jnp.int32, (count, HD), 0) + base
        return (starts <= pos) & (pos < ends)

    for t in range(0, WIN, HALF):
        key_doc[t:t + HALF] = jnp.where(inside(HALF, ctx * TOK - REACH + t), 1.0, 0.0).astype(jnp.bfloat16)
    for t in range(0, TOK, HALF):
        query_doc[t:t + HALF] = jnp.where(inside(HALF, ctx * TOK + t), 0.0, -1e30).astype(jnp.bfloat16)

    causal = (lax.broadcasted_iota(jnp.int32, (HALF, HALF), 0)
              <= lax.broadcasted_iota(jnp.int32, (HALF, HALF), 1))

    def fold(x):
        return jnp.sum(x.reshape(x.shape[0] // 8, 8, x.shape[1]), axis=0)

    slots = {(0, 0): 0, (0, 1): 2, (1, 0): 4, (1, 1): 0}

    def part(s, c, j, low, high):
        slot = slots[s, j] + c
        score, wgrad = scores.at[slot], wgrads.at[slot]
        rows = pl.ds(c * HALF + low, high - low)
        keyed = jnp.concatenate([win[0, s, rows], key_doc[rows]], axis=1)
        asked = jnp.concatenate([qo[0, s, c, j], query_doc[c * HALF:(c + 1) * HALF]], axis=1)
        score[low:high] = lax.dot_general(keyed, asked, NT, preferred_element_type=jnp.float32)
        wgrad[low:high] = lax.dot_general(
            win[1, s, rows], qo[1, s, c, j], NT, preferred_element_type=jnp.float32)
        if high == SPAN:
            score[REACH:SPAN] = jnp.where(causal, score[REACH:SPAN], -1e30)
        peak = None
        for t in range(low, high, TILE):
            x = score[t:t + TILE]
            x = jnp.max(x.reshape(TILE // 8, 8, HALF), axis=0)
            peak = x if peak is None else jnp.maximum(peak, x)
        top = jnp.max(peak, axis=0, keepdims=True)
        total = jnp.zeros((8, HALF), jnp.float32)
        dots = jnp.zeros((8, HALF), jnp.float32)
        for t in range(low, high, TILE):
            e = jnp.exp2((score[t:t + TILE] - top) * (SCALE * LOG2E))
            score[t:t + TILE] = e
            total += fold(e)
            dots += fold(e * wgrad[t:t + TILE])
        return top, jnp.sum(total, axis=0, keepdims=True), jnp.sum(dots, axis=0, keepdims=True)

    def early(s, c, j):
        slot = slots[s, j] + c
        for row, value in enumerate(part(s, c, j, TOK - c * HALF, SPAN)):
            stats[slot, row:row + 1] = value

    def late(s, c, j):
        slot, border = slots[s, j] + c, TOK - c * HALF
        score, wgrad = scores.at[slot], wgrads.at[slot]
        far_top, far_total, far_dots = part(s, c, j, 0, border)
        near_top, near_total, near_dots = (stats[slot, row:row + 1] for row in range(3))
        top = jnp.maximum(far_top, near_top)
        far_scale = jnp.exp2((far_top - top) * (SCALE * LOG2E))
        near_scale = jnp.exp2((near_top - top) * (SCALE * LOG2E))
        inverse = 1.0 / (far_total * far_scale + near_total * near_scale)
        delta = (far_dots * far_scale + near_dots * near_scale) * inverse
        at = pl.ds(c * TOK + j * HALF, HALF)
        for t in range(0, SPAN, TILE):
            weights = score[t:t + TILE] * ((far_scale if t < border else near_scale) * inverse)
            rows = slice(c * HALF + t, c * HALF + t + TILE)
            pd[s, 1, rows, at] = weights.astype(jnp.bfloat16)
            pd[s, 0, rows, at] = (weights * (wgrad[t:t + TILE] - delta)).astype(jnp.bfloat16)

    def query_grads(s):
        for c in halves:
            rows = pl.ds(c * HALF, SPAN)
            found = lax.dot_general(
                pd[s, 0, rows, c * TOK:(c + 1) * TOK], win[0, s, rows], TN, preferred_element_type=jnp.float32)
            dqs[s, :, c] = (found * SCALE).astype(jnp.bfloat16).reshape(2, HALF, HD)
        dq_far[s].start()
        dq_near[s].start()

    pieces = (((0, HALF, 0, 1), (HALF, TOK, 0, 2)), ((TOK, SPAN, 0, 2), (SPAN, WIN, 1, 2)))

    def product(kind, s, piece):
        low, high, c0, c1 = piece
        right = qo[kind, s, c0:c1].reshape(((c1 - c0) * TOK, HD))
        return mm(pd[s, kind, low:high, c0 * TOK:c1 * TOK], right) * jnp.where(kind == 0, SCALE, 1.0)

    def theirs(s, h):
        for piece in pieces[h]:
            mate_out[s, piece[0]:piece[1]] = product(other, s, piece).astype(jnp.bfloat16)
        mt[s][h].start()

    def ours(s, h):
        for piece in pieces[h]:
            mine[piece[0]:piece[1]] = product(core, s, piece)

    def outer(s):
        theirs(s, 0)
        ours(s, 0)
        theirs(s, 1)
        mt[s][0].wait_recv()
        for q in range(4):
            at = slice(q * 128, (q + 1) * 128)
            r2_out[s, at] = (mine[at] + mate_in[s, at].astype(jnp.float32)).astype(jnp.bfloat16)
            r2[s][q].start()
        ours(s, 1)
        mt[s][1].wait_recv()
        hop1[s] = mine[TOK:REACH] + mate_in[s, TOK:REACH].astype(jnp.float32)
        h0_out[s] = (mine[REACH:WIN] + mate_in[s, REACH:WIN].astype(jnp.float32)).astype(jnp.bfloat16)
        for q in range(4):
            @pl.when(head != q)
            def _(q=q):
                h0[s][q].start()

            @pl.when(head == q)
            def _(q=q):
                pltpu.make_async_copy(h0_out.at[s, quarters[q]], h0_in.at[s, q], h0_r.at[s, q]).start()

    def middle(s):
        for q in range(4):
            at = slice(q * 128, (q + 1) * 128)
            r2[s][q].wait_recv()
            r1_out[s, at] = (hop1[s, at] + r2_in[s, at].astype(jnp.float32)).astype(jnp.bfloat16)
            r1[s][q].start()

    def finish(s):
        for h in range(4):
            h0_from[s][h].wait_recv()
            r1_from[s][h].wait_recv()
            out = (dk_ref, dv_ref)[h % 2]
            g = (h // 2) * 2 + s
            out[:, g * HD:(g + 1) * HD] = (
                h0_in[s, h].astype(jnp.float32) + r1_in[s, h].astype(jnp.float32)).astype(jnp.bfloat16)

    def forward(s):
        z1[s].wait_recv()
        if s == 1:
            either(z2[1], z2_relayed)
        else:
            z2[s].start()
        m1[s].start()

    def pass_on(k):
        @pl.when(at_end)
        def _():
            (z1_relayed, z2_relayed)[k].wait_recv()
            passed[k].start()

    def arrive(s):
        z2[s].wait_recv()
        m2[s].start()

    forward(0)
    m1_in[0].wait_recv()
    early(0, 0, 0)
    early(0, 1, 0)

    @pl.when(jnp.logical_not(at_start))
    def _():
        forward(1)

    pass_on(0)

    @pl.when(jnp.logical_not(at_start))
    def _():
        m1_in[1].wait_recv()
        early(1, 0, 0)
        early(1, 1, 0)

    for copy in xq[0]:
        copy.wait_recv()
    early(0, 0, 1)
    arrive(0)
    early(0, 1, 1)
    m2_in[0].wait_recv()
    late(0, 0, 0)

    @pl.when(at_start)
    def _():
        forward(1)

    late(0, 1, 0)
    pass_on(1)
    late(0, 0, 1)
    late(0, 1, 1)
    outer(0)

    @pl.when(at_start)
    def _():
        m1_in[1].wait_recv()
        early(1, 0, 0)
        early(1, 1, 0)

    for copy in xq[1]:
        copy.wait_recv()
    early(1, 0, 1)
    arrive(1)
    early(1, 1, 1)
    query_grads(0)
    m2_in[1].wait_recv()
    late(1, 0, 0)
    late(1, 1, 0)
    middle(0)
    late(1, 0, 1)
    late(1, 1, 1)
    outer(1)
    query_grads(1)
    middle(1)
    finish(0)
    finish(1)

    @pl.when(at_end)
    def _():
        for copy in passed:
            copy.wait_send()

    for s in stages:
        for copy in (z1[s], z2[s], m1[s], m2[s], *xq[s], *mt[s], *r2[s], *r1[s], dq_far[s]):
            copy.wait_send()
        for q in range(4):
            @pl.when(head != q)
            def _(q=q):
                h0[s][q].wait_send()
        dq_far_in[s].wait_recv()
        dq_near[s].wait()


def local(ctx_size, queries, keys, values, grad_out, doc_lengths):
    bf16, f32 = jnp.bfloat16, jnp.float32
    anywhere = pl.BlockSpec(memory_space=pl.ANY)
    pair = pltpu.SemaphoreType.DMA((STAGES,))
    quad = pltpu.SemaphoreType.DMA((STAGES, 2))
    eight = pltpu.SemaphoreType.DMA((STAGES, 4))
    block16 = pltpu.VMEM((STAGES, TOK, HD), bf16)
    heads16 = pltpu.VMEM((STAGES, 4, 128, HD), bf16)
    dq, dk, dv = pl.pallas_call(
        lambda *refs: kernel(ctx_size, *refs),
        out_shape=(
            pltpu.VMEM((2, HALF, KVH * HD), bf16),
            pltpu.VMEM((128, KVH * HD), bf16),
            pltpu.VMEM((128, KVH * HD), bf16),
        ),
        in_specs=[anywhere] * 4 + [pl.BlockSpec(memory_space=pltpu.VMEM)],
        out_specs=(pl.BlockSpec(memory_space=pltpu.VMEM), pl.BlockSpec(memory_space=pltpu.VMEM), pl.BlockSpec(memory_space=pltpu.VMEM)),
        scratch_shapes=[
            pltpu.VMEM((2, STAGES, WIN, HD), bf16),
            pltpu.VMEM((2, STAGES, 2, 2, HALF, HD), bf16),
            pltpu.VMEM((STAGES, 2, WIN, 2 * TOK), bf16),
            pltpu.VMEM((6, SPAN, HALF), f32),
            pltpu.VMEM((6, SPAN, HALF), f32),
            pltpu.VMEM((6, 8, HALF), f32),
            pltpu.VMEM((WIN, HD), f32),
            pltpu.VMEM((STAGES, 2, 2, HALF, HD), bf16),
            pltpu.VMEM((WIN, HD), bf16),
            pltpu.VMEM((TOK, HD), bf16),
            pltpu.VMEM((STAGES, WIN, HD), bf16),
            pltpu.VMEM((STAGES, WIN, HD), bf16),
            pltpu.VMEM((STAGES, TOK, HD), f32),
            block16, block16, block16, heads16, block16, heads16,
            block16,
            pltpu.SemaphoreType.DMA((4, STAGES)),
            pair, pair, pair, pair, pair, pair, pair, pair,
            quad, quad,
            quad, quad, eight, eight, eight, eight, pair, pair, pair,
            eight, eight,
            pair, pair,
        ],
        compiler_params=pltpu.CompilerParams(
            collective_id=0, has_side_effects=True, vmem_limit_bytes=56 * 2**20),
        cost_estimate=pl.CostEstimate(
            flops=10 * 4 * TOK * SPAN * HD, bytes_accessed=4 * 2**20, transcendentals=4 * TOK * SPAN),
        name="attention_backward",
    )(queries.reshape(2, HALF, KVH * HD), keys, values, grad_out.reshape(2, HALF, KVH * HD),
      doc_lengths.reshape(1, 64))
    return dq.reshape(TOK, 1, KVH * HD), dk, dv


def solution(mesh):
    placed = (P("ctx", "head", None), P("ctx", None), P("ctx", None), P("ctx", "head", None), P())
    ctx_size = mesh.shape["ctx"]
    return jax.shard_map(
        lambda *args: local(ctx_size, *args),
        mesh=mesh,
        in_specs=placed,
        out_specs=(P("ctx", "head", None), P(("ctx", "head"), None), P(("ctx", "head"), None)),
        check_vma=False,
    )
```

```python
import math

import jax
import jax.numpy as jnp
from jax import lax
from jax.experimental import pallas as pl
from jax.experimental.pallas import tpu as pltpu
from jax.sharding import PartitionSpec as P

HD = 128
KVH = 4
TOK = 512
HALF = 256
REACH = 1024
WIN = REACH + TOK
SPAN = REACH + HALF
TILE = 64
STAGES = 2
ROW = 8
MESH = pl.DeviceIdType.MESH
SCALE = 1.0 / math.sqrt(HD)
LOG2E = math.log2(math.e)
NT = (((1,), (1,)), ((), ()))
TN = (((0,), (0,)), ((), ()))


def mm(a, b):
    return jnp.dot(a, b, preferred_element_type=jnp.float32)


def kernel(
    ctx_size,
    q_ref, k_ref, v_ref, g_ref, len_ref,
    dq_ref, dk_ref, dv_ref,
    win, qo, pd, scores, wgrads, stats, mine, dqs, key_doc, query_doc,
    mate_out, mate_in, hop1, r2_out, r2_in, r1_out, r1_in, h0_out, h0_in, relay,
    load_sem, z1_s, z1_r, z2_s, z2_r, m1_s, m1_r, m2_s, m2_r, x_s, x_r,
    mt_s, mt_r, r2_s, r2_r, r1_s, r1_r, dq_s, dq_r, dq_l, h0_s, h0_r, relay_s, relay_r,
):
    ctx = lax.axis_index("ctx")
    head = lax.axis_index("head")
    core = lax.rem(head, 2)
    chip = head // 2
    other = 1 - core
    nxt = (lax.rem(ctx + 1, ctx_size), head)
    prv = (lax.rem(ctx + ctx_size - 1, ctx_size), head)
    mate = (ctx, chip * 2 + other)
    partner = (ctx, (1 - chip) * 2 + core)
    diagonal = (ctx, (1 - chip) * 2 + other)
    stages, halves = range(STAGES), range(2)
    place = lax.rem(ctx, ROW)
    at_start, at_end = place == 0, place == ROW - 1

    def near(steps):
        return (lax.rem(ctx + ctx_size + steps, ctx_size), head)

    relay_to, relay_from, relay_down, relay_up = near(ROW), near(-ROW), near(1 - ROW), near(ROW - 1)

    def cols(owner, s):
        return pl.ds(pl.multiple_of((owner * 2 + s) * HD, HD), HD)

    def remote(src, dst, send, recv, device):
        return pltpu.make_async_remote_copy(
            src_ref=src, dst_ref=dst, send_sem=send, recv_sem=recv,
            device_id=device, device_id_type=MESH,
        )

    own_rows = pl.ds(REACH, TOK)
    hop1_rows = pl.ds(TOK, TOK)
    hop2_rows = pl.ds(0, TOK)

    loads = []
    for s in stages:
        for kind, ref in ((0, k_ref), (1, v_ref)):
            loads.append(pltpu.make_async_copy(
                ref.at[:, cols(chip, s)], win.at[kind, s, own_rows], load_sem.at[kind, s]))
        for kind, ref in ((0, q_ref), (1, g_ref)):
            loads.append(pltpu.make_async_copy(
                ref.at[:, :, cols(chip, s)], qo.at[kind, s, :, 0], load_sem.at[2 + kind, s]))
    for load in loads:
        load.start()

    barrier = pltpu.get_barrier_semaphore()
    for device in (mate, partner, diagonal, *[(nxt[0], h) for h in range(4)], *[(prv[0], h) for h in range(4)]):
        pl.semaphore_signal(barrier, 1, device_id=device, device_id_type=MESH)

    @pl.when(at_end)
    def _():
        for device in (relay_to, relay_from, relay_down):
            pl.semaphore_signal(barrier, 1, device_id=device, device_id_type=MESH)

    @pl.when(at_start)
    def _():
        pl.semaphore_signal(barrier, 1, device_id=relay_up, device_id_type=MESH)

    for load in loads:
        load.wait()
    pl.semaphore_wait(barrier, 11 + 3 * (place // (ROW - 1)) + (ROW - 1 - place) // (ROW - 1))

    z1 = [remote(win.at[core, s, own_rows], win.at[core, s, hop1_rows], z1_s.at[s], z1_r.at[s], nxt) for s in stages]
    z2 = [remote(win.at[core, s, hop1_rows], win.at[core, s, hop2_rows], z2_s.at[s], z2_r.at[s], nxt) for s in stages]
    z1_relayed = remote(win.at[core, 1, own_rows], relay.at[0], z1_s.at[1], relay_r.at[0], relay_to)
    z2_relayed = remote(win.at[core, 1, hop1_rows], relay.at[1], z2_s.at[1], relay_r.at[1], relay_to)
    passed = [remote(relay.at[k], win.at[core, 1, rows], relay_s.at[k], sem.at[1], relay_down)
              for k, (rows, sem) in enumerate(((hop1_rows, z1_r), (hop2_rows, z2_r)))]
    m1 = [remote(win.at[core, s, hop1_rows], win.at[core, s, hop1_rows], m1_s.at[s], m1_r.at[s], mate)
          for s in stages]
    m1_in = [remote(win.at[other, s, hop1_rows], win.at[other, s, hop1_rows], m1_s.at[s], m1_r.at[s], mate)
             for s in stages]
    m2 = [remote(win.at[core, s, hop2_rows], win.at[core, s, hop2_rows], m2_s.at[s], m2_r.at[s], mate)
          for s in stages]
    m2_in = [remote(win.at[other, s, hop2_rows], win.at[other, s, hop2_rows], m2_s.at[s], m2_r.at[s], mate)
             for s in stages]
    xq = [[remote(ref.at[:, :, cols(1 - chip, s)], qo.at[kind, s, :, 1], x_s.at[kind, s], x_r.at[kind, s], partner)
           for kind, ref in ((0, q_ref), (1, g_ref))] for s in stages]
    mate_rows = (hop2_rows, pl.ds(TOK, 2 * TOK))
    mt = [[remote(mate_out.at[s, mate_rows[h]], mate_in.at[s, mate_rows[h]], mt_s.at[s, h], mt_r.at[s, h], mate)
           for h in halves] for s in stages]
    quarters = [pl.ds(q * 128, 128) for q in range(4)]
    r2 = [[remote(r2_out.at[s, rows], r2_in.at[s, rows], r2_s.at[s, q], r2_r.at[s, q], prv)
           for q, rows in enumerate(quarters)] for s in stages]
    r1 = [[remote(r1_out.at[s, rows], r1_in.at[s, head], r1_s.at[s, q], r1_r.at[s, head], (prv[0], q))
           for q, rows in enumerate(quarters)] for s in stages]
    r1_from = [[remote(r1_out.at[s, quarters[0]], r1_in.at[s, h], r1_s.at[s, 0], r1_r.at[s, h], prv)
                for h in range(4)] for s in stages]
    h0 = [[remote(h0_out.at[s, rows], h0_in.at[s, head], h0_s.at[s, q], h0_r.at[s, head], (ctx, q))
           for q, rows in enumerate(quarters)] for s in stages]
    h0_from = [[remote(h0_out.at[s, quarters[0]], h0_in.at[s, h], h0_s.at[s, 0], h0_r.at[s, h], mate)
                for h in range(4)] for s in stages]
    dq_far = [remote(dqs.at[s, 1], dq_ref.at[:, :, cols(chip, s)], dq_s.at[s], dq_r.at[s], partner)
              for s in stages]
    dq_far_in = [remote(dqs.at[s, 1], dq_ref.at[:, :, cols(1 - chip, s)], dq_s.at[s], dq_r.at[s], partner)
                 for s in stages]
    dq_near = [pltpu.make_async_copy(dqs.at[s, 0], dq_ref.at[:, :, cols(chip, s)], dq_l.at[s])
               for s in stages]

    z1[0].start()

    def either(direct, relayed):
        @pl.when(at_end)
        def _():
            relayed.start()

        @pl.when(jnp.logical_not(at_end))
        def _():
            direct.start()

    either(z1[1], z1_relayed)
    for copy in xq[0]:
        copy.start()

    @pl.when(jnp.logical_not(at_start | at_end))
    def _():
        for copy in xq[1]:
            copy.start()


    lengths = len_ref[...]
    upto = jnp.where(
        lax.broadcasted_iota(jnp.int32, (64, HD), 0) <= lax.broadcasted_iota(jnp.int32, (64, HD), 1), 1.0, 0.0
    ).astype(jnp.bfloat16)

    def ends_of(part):
        rows = jnp.broadcast_to(part, (16, 64)).astype(jnp.float32).astype(jnp.bfloat16)
        return mm(rows, upto)[0:1]

    ends = (ends_of(lengths >> 5) * 32.0 + ends_of(lengths & 31)).astype(jnp.int32)
    wide = (16, 64)
    before = jnp.where(
        lax.broadcasted_iota(jnp.int32, (64, HD), 0) < lax.broadcasted_iota(jnp.int32, (64, HD), 1), 1.0, 0.0
    ).astype(jnp.bfloat16)

    def starts_of(part):
        rows = jnp.broadcast_to(part, wide).astype(jnp.float32).astype(jnp.bfloat16)
        return mm(rows, before)[0:1]

    starts = (starts_of(lengths >> 5) * 32.0 + starts_of(lengths & 31)).astype(jnp.int32)
    lane = lax.broadcasted_iota(jnp.int32, (1, HD), 1)
    starts = jnp.where(lane == 64, -WIN, starts)
    ends = jnp.where(lane == 64, 0, ends)

    def inside(count, base):
        pos = lax.broadcasted_iota(jnp.int32, (count, HD), 0) + base
        return (starts <= pos) & (pos < ends)

    for t in range(0, WIN, HALF):
        key_doc[t:t + HALF] = jnp.where(inside(HALF, ctx * TOK - REACH + t), 1.0, 0.0).astype(jnp.bfloat16)
    for t in range(0, TOK, HALF):
        query_doc[t:t + HALF] = jnp.where(inside(HALF, ctx * TOK + t), 0.0, -1e30).astype(jnp.bfloat16)

    causal = (lax.broadcasted_iota(jnp.int32, (HALF, HALF), 0)
              <= lax.broadcasted_iota(jnp.int32, (HALF, HALF), 1))

    def fold(x):
        return jnp.sum(x.reshape(x.shape[0] // 8, 8, x.shape[1]), axis=0)

    slots = {(0, 0): 0, (0, 1): 2, (1, 0): 4, (1, 1): 0}

    def part(s, c, j, low, high):
        slot = slots[s, j] + c
        score, wgrad = scores.at[slot], wgrads.at[slot]
        rows = pl.ds(c * HALF + low, high - low)
        keyed = jnp.concatenate([win[0, s, rows], key_doc[rows]], axis=1)
        asked = jnp.concatenate([qo[0, s, c, j], query_doc[c * HALF:(c + 1) * HALF]], axis=1)
        score[low:high] = lax.dot_general(keyed, asked, NT, preferred_element_type=jnp.float32)
        wgrad[low:high] = lax.dot_general(
            win[1, s, rows], qo[1, s, c, j], NT, preferred_element_type=jnp.float32)
        if high == SPAN:
            score[REACH:SPAN] = jnp.where(causal, score[REACH:SPAN], -1e30)
        peak = None
        for t in range(low, high, TILE):
            x = score[t:t + TILE]
            x = jnp.max(x.reshape(TILE // 8, 8, HALF), axis=0)
            peak = x if peak is None else jnp.maximum(peak, x)
        top = jnp.max(peak, axis=0, keepdims=True)
        total = jnp.zeros((8, HALF), jnp.float32)
        dots = jnp.zeros((8, HALF), jnp.float32)
        for t in range(low, high, TILE):
            e = jnp.exp2((score[t:t + TILE] - top) * (SCALE * LOG2E))
            score[t:t + TILE] = e
            total += fold(e)
            dots += fold(e * wgrad[t:t + TILE])
        return top, jnp.sum(total, axis=0, keepdims=True), jnp.sum(dots, axis=0, keepdims=True)

    def early(s, c, j):
        slot = slots[s, j] + c
        for row, value in enumerate(part(s, c, j, TOK - c * HALF, SPAN)):
            stats[slot, row:row + 1] = value

    def late(s, c, j):
        slot, border = slots[s, j] + c, TOK - c * HALF
        score, wgrad = scores.at[slot], wgrads.at[slot]
        far_top, far_total, far_dots = part(s, c, j, 0, border)
        near_top, near_total, near_dots = (stats[slot, row:row + 1] for row in range(3))
        top = jnp.maximum(far_top, near_top)
        far_scale = jnp.exp2((far_top - top) * (SCALE * LOG2E))
        near_scale = jnp.exp2((near_top - top) * (SCALE * LOG2E))
        inverse = 1.0 / (far_total * far_scale + near_total * near_scale)
        delta = (far_dots * far_scale + near_dots * near_scale) * inverse
        at = pl.ds(c * TOK + j * HALF, HALF)
        for t in range(0, SPAN, TILE):
            weights = score[t:t + TILE] * ((far_scale if t < border else near_scale) * inverse)
            rows = slice(c * HALF + t, c * HALF + t + TILE)
            pd[s, 1, rows, at] = weights.astype(jnp.bfloat16)
            pd[s, 0, rows, at] = (weights * (wgrad[t:t + TILE] - delta)).astype(jnp.bfloat16)

    def query_grads(s):
        for c in halves:
            rows = pl.ds(c * HALF, SPAN)
            found = lax.dot_general(
                pd[s, 0, rows, c * TOK:(c + 1) * TOK], win[0, s, rows], TN, preferred_element_type=jnp.float32)
            dqs[s, :, c] = (found * SCALE).astype(jnp.bfloat16).reshape(2, HALF, HD)
        dq_far[s].start()
        dq_near[s].start()

    pieces = (((0, HALF, 0, 1), (HALF, TOK, 0, 2)), ((TOK, SPAN, 0, 2), (SPAN, WIN, 1, 2)))

    def product(kind, s, piece):
        low, high, c0, c1 = piece
        right = qo[kind, s, c0:c1].reshape(((c1 - c0) * TOK, HD))
        return mm(pd[s, kind, low:high, c0 * TOK:c1 * TOK], right) * jnp.where(kind == 0, SCALE, 1.0)

    def theirs(s, h):
        for piece in pieces[h]:
            mate_out[s, piece[0]:piece[1]] = product(other, s, piece).astype(jnp.bfloat16)
        mt[s][h].start()

    def ours(s, h):
        for piece in pieces[h]:
            mine[piece[0]:piece[1]] = product(core, s, piece)

    def outer(s):
        theirs(s, 0)
        ours(s, 0)
        theirs(s, 1)
        mt[s][0].wait_recv()
        for q in range(4):
            at = slice(q * 128, (q + 1) * 128)
            r2_out[s, at] = (mine[at] + mate_in[s, at].astype(jnp.float32)).astype(jnp.bfloat16)
            r2[s][q].start()
        ours(s, 1)
        mt[s][1].wait_recv()
        hop1[s] = mine[TOK:REACH] + mate_in[s, TOK:REACH].astype(jnp.float32)
        h0_out[s] = (mine[REACH:WIN] + mate_in[s, REACH:WIN].astype(jnp.float32)).astype(jnp.bfloat16)
        for q in range(4):
            @pl.when(head != q)
            def _(q=q):
                h0[s][q].start()

            @pl.when(head == q)
            def _(q=q):
                pltpu.make_async_copy(h0_out.at[s, quarters[q]], h0_in.at[s, q], h0_r.at[s, q]).start()

    def middle(s):
        for q in range(4):
            at = slice(q * 128, (q + 1) * 128)
            r2[s][q].wait_recv()
            r1_out[s, at] = (hop1[s, at] + r2_in[s, at].astype(jnp.float32)).astype(jnp.bfloat16)
            r1[s][q].start()

    def finish(s):
        for h in range(4):
            h0_from[s][h].wait_recv()
            r1_from[s][h].wait_recv()
            out = (dk_ref, dv_ref)[h % 2]
            g = (h // 2) * 2 + s
            out[:, g * HD:(g + 1) * HD] = (
                h0_in[s, h].astype(jnp.float32) + r1_in[s, h].astype(jnp.float32)).astype(jnp.bfloat16)

    def forward(s):
        z1[s].wait_recv()
        if s == 1:
            either(z2[1], z2_relayed)
        else:
            z2[s].start()
        m1[s].start()

    def pass_on(k):
        @pl.when(at_end)
        def _():
            (z1_relayed, z2_relayed)[k].wait_recv()
            passed[k].start()

    def arrive(s):
        z2[s].wait_recv()
        m2[s].start()

    forward(0)
    m1_in[0].wait_recv()
    early(0, 0, 0)
    early(0, 1, 0)

    @pl.when(jnp.logical_not(at_start))
    def _():
        forward(1)

    pass_on(0)

    @pl.when(jnp.logical_not(at_start))
    def _():
        m1_in[1].wait_recv()
        early(1, 0, 0)
        early(1, 1, 0)

    for copy in xq[0]:
        copy.wait_recv()

    @pl.when(at_start | at_end)
    def _():
        for copy in xq[1]:
            copy.start()

    early(0, 0, 1)
    arrive(0)
    early(0, 1, 1)
    m2_in[0].wait_recv()
    late(0, 0, 0)

    @pl.when(at_start)
    def _():
        forward(1)

    late(0, 1, 0)
    pass_on(1)
    late(0, 0, 1)
    late(0, 1, 1)
    outer(0)

    @pl.when(at_start)
    def _():
        m1_in[1].wait_recv()
        early(1, 0, 0)
        early(1, 1, 0)

    for copy in xq[1]:
        copy.wait_recv()
    early(1, 0, 1)
    arrive(1)
    early(1, 1, 1)
    query_grads(0)
    m2_in[1].wait_recv()
    late(1, 0, 0)
    late(1, 1, 0)
    middle(0)
    late(1, 0, 1)
    late(1, 1, 1)
    outer(1)
    query_grads(1)
    middle(1)
    finish(0)
    finish(1)

    @pl.when(at_end)
    def _():
        for copy in passed:
            copy.wait_send()

    for s in stages:
        for copy in (z1[s], z2[s], m1[s], m2[s], *xq[s], *mt[s], *r2[s], *r1[s], dq_far[s]):
            copy.wait_send()
        for q in range(4):
            @pl.when(head != q)
            def _(q=q):
                h0[s][q].wait_send()
        dq_far_in[s].wait_recv()
        dq_near[s].wait()


def write_out(*refs):
    sources, targets, sem = refs[0:3], refs[3:6], refs[6]
    copies = [pltpu.make_async_copy(source, target, sem.at[i])
              for i, (source, target) in enumerate(zip(sources, targets, strict=True))]
    for copy in copies:
        copy.start()
    for copy in copies:
        copy.wait()


def local(ctx_size, queries, keys, values, grad_out, doc_lengths):
    bf16, f32 = jnp.bfloat16, jnp.float32
    anywhere = pl.BlockSpec(memory_space=pl.ANY)
    pair = pltpu.SemaphoreType.DMA((STAGES,))
    quad = pltpu.SemaphoreType.DMA((STAGES, 2))
    eight = pltpu.SemaphoreType.DMA((STAGES, 4))
    block16 = pltpu.VMEM((STAGES, TOK, HD), bf16)
    heads16 = pltpu.VMEM((STAGES, 4, 128, HD), bf16)
    dq, dk, dv = pl.pallas_call(
        lambda *refs: kernel(ctx_size, *refs),
        out_shape=(
            pltpu.VMEM((2, HALF, KVH * HD), bf16),
            pltpu.VMEM((128, KVH * HD), bf16),
            pltpu.VMEM((128, KVH * HD), bf16),
        ),
        in_specs=[anywhere] * 4 + [pl.BlockSpec(memory_space=pltpu.VMEM)],
        out_specs=(pl.BlockSpec(memory_space=pltpu.VMEM), pl.BlockSpec(memory_space=pltpu.VMEM), pl.BlockSpec(memory_space=pltpu.VMEM)),
        scratch_shapes=[
            pltpu.VMEM((2, STAGES, WIN, HD), bf16),
            pltpu.VMEM((2, STAGES, 2, 2, HALF, HD), bf16),
            pltpu.VMEM((STAGES, 2, WIN, 2 * TOK), bf16),
            pltpu.VMEM((6, SPAN, HALF), f32),
            pltpu.VMEM((6, SPAN, HALF), f32),
            pltpu.VMEM((6, 8, HALF), f32),
            pltpu.VMEM((WIN, HD), f32),
            pltpu.VMEM((STAGES, 2, 2, HALF, HD), bf16),
            pltpu.VMEM((WIN, HD), bf16),
            pltpu.VMEM((TOK, HD), bf16),
            pltpu.VMEM((STAGES, WIN, HD), bf16),
            pltpu.VMEM((STAGES, WIN, HD), bf16),
            pltpu.VMEM((STAGES, TOK, HD), f32),
            block16, block16, block16, heads16, block16, heads16,
            block16,
            pltpu.SemaphoreType.DMA((4, STAGES)),
            pair, pair, pair, pair, pair, pair, pair, pair,
            quad, quad,
            quad, quad, eight, eight, eight, eight, pair, pair, pair,
            eight, eight,
            pair, pair,
        ],
        compiler_params=pltpu.CompilerParams(
            collective_id=0, has_side_effects=True, vmem_limit_bytes=56 * 2**20),
        cost_estimate=pl.CostEstimate(
            flops=10 * 4 * TOK * SPAN * HD, bytes_accessed=4 * 2**20, transcendentals=4 * TOK * SPAN),
        name="attention_backward",
    )(queries.reshape(2, HALF, KVH * HD), keys, values, grad_out.reshape(2, HALF, KVH * HD),
      doc_lengths.reshape(1, 64))
    dq, dk, dv = pl.pallas_call(
        write_out,
        out_shape=tuple(jax.ShapeDtypeStruct(x.shape, bf16) for x in (dq, dk, dv)),
        in_specs=[anywhere] * 3,
        out_specs=(anywhere,) * 3,
        scratch_shapes=[pltpu.SemaphoreType.DMA((3,))],
        compiler_params=pltpu.CompilerParams(vmem_limit_bytes=4 * 2**20),
        name="write_out",
    )(dq, dk, dv)
    return dq.reshape(TOK, 1, KVH * HD), dk, dv


def solution(mesh):
    placed = (P("ctx", "head", None), P("ctx", None), P("ctx", None), P("ctx", "head", None), P())
    ctx_size = mesh.shape["ctx"]
    return jax.shard_map(
        lambda *args: local(ctx_size, *args),
        mesh=mesh,
        in_specs=placed,
        out_specs=(P("ctx", "head", None), P(("ctx", "head"), None), P(("ctx", "head"), None)),
        check_vma=False,
    )
```

```python
import math

import jax
import jax.numpy as jnp
from jax import lax
from jax.experimental import pallas as pl
from jax.experimental.pallas import tpu as pltpu
from jax.sharding import PartitionSpec as P

HD = 128
KVH = 4
TOK = 512
HALF = 256
REACH = 1024
WIN = REACH + TOK
SPAN = REACH + HALF
TILE = 64
STAGES = 2
ROW = 8
MESH = pl.DeviceIdType.MESH
SCALE = 1.0 / math.sqrt(HD)
LOG2E = math.log2(math.e)
NT = (((1,), (1,)), ((), ()))
TN = (((0,), (0,)), ((), ()))


def mm(a, b):
    return jnp.dot(a, b, preferred_element_type=jnp.float32)


def kernel(
    ctx_size,
    q_ref, k_ref, v_ref, g_ref, len_ref,
    dq_ref, dk_ref, dv_ref,
    win, qo, pd, scores, wgrads, stats, mine, dqs, key_doc, query_doc,
    mate_out, mate_in, hop1, r2_out, r2_in, r1_out, r1_in, h0_out, h0_in, relay,
    load_sem, z1_s, z1_r, z2_s, z2_r, m1_s, m1_r, m2_s, m2_r, x_s, x_r,
    mt_s, mt_r, r2_s, r2_r, r1_s, r1_r, dq_s, dq_r, dq_l, h0_s, h0_r, relay_s, relay_r,
):
    ctx = lax.axis_index("ctx")
    head = lax.axis_index("head")
    core = lax.rem(head, 2)
    chip = head // 2
    other = 1 - core
    nxt = (lax.rem(ctx + 1, ctx_size), head)
    prv = (lax.rem(ctx + ctx_size - 1, ctx_size), head)
    mate = (ctx, chip * 2 + other)
    partner = (ctx, (1 - chip) * 2 + core)
    diagonal = (ctx, (1 - chip) * 2 + other)
    stages, halves = range(STAGES), range(2)
    place = lax.rem(ctx, ROW)
    at_start, at_end = place == 0, place == ROW - 1

    def near(steps):
        return (lax.rem(ctx + ctx_size + steps, ctx_size), head)

    relay_to, relay_from, relay_down, relay_up = near(ROW), near(-ROW), near(1 - ROW), near(ROW - 1)

    def cols(owner, s):
        return pl.ds(pl.multiple_of((owner * 2 + s) * HD, HD), HD)

    def remote(src, dst, send, recv, device):
        return pltpu.make_async_remote_copy(
            src_ref=src, dst_ref=dst, send_sem=send, recv_sem=recv,
            device_id=device, device_id_type=MESH,
        )

    own_rows = pl.ds(REACH, TOK)
    hop1_rows = pl.ds(TOK, TOK)
    hop2_rows = pl.ds(0, TOK)

    loads = []
    for s in stages:
        for kind, ref in ((0, k_ref), (1, v_ref)):
            loads.append(pltpu.make_async_copy(
                ref.at[:, cols(chip, s)], win.at[kind, s, own_rows], load_sem.at[kind, s]))
        for kind, ref in ((0, q_ref), (1, g_ref)):
            loads.append(pltpu.make_async_copy(
                ref.at[:, :, cols(chip, s)], qo.at[kind, s, :, 0], load_sem.at[2 + kind, s]))
    for load in loads:
        load.start()

    barrier = pltpu.get_barrier_semaphore()
    for device in (mate, partner, diagonal, *[(nxt[0], h) for h in range(4)], *[(prv[0], h) for h in range(4)]):
        pl.semaphore_signal(barrier, 1, device_id=device, device_id_type=MESH)

    @pl.when(at_end)
    def _():
        for device in (relay_to, relay_from, relay_down):
            pl.semaphore_signal(barrier, 1, device_id=device, device_id_type=MESH)

    @pl.when(at_start)
    def _():
        pl.semaphore_signal(barrier, 1, device_id=relay_up, device_id_type=MESH)

    for load in loads:
        load.wait()
    pl.semaphore_wait(barrier, 11 + 3 * (place // (ROW - 1)) + (ROW - 1 - place) // (ROW - 1))

    z1 = [remote(win.at[core, s, own_rows], win.at[core, s, hop1_rows], z1_s.at[s], z1_r.at[s], nxt) for s in stages]
    z2 = [remote(win.at[core, s, hop1_rows], win.at[core, s, hop2_rows], z2_s.at[s], z2_r.at[s], nxt) for s in stages]
    z1_relayed = remote(win.at[core, 1, own_rows], relay.at[0], z1_s.at[1], relay_r.at[0], relay_to)
    z2_relayed = remote(win.at[core, 1, hop1_rows], relay.at[1], z2_s.at[1], relay_r.at[1], relay_to)
    passed = [remote(relay.at[k], win.at[core, 1, rows], relay_s.at[k], sem.at[1], relay_down)
              for k, (rows, sem) in enumerate(((hop1_rows, z1_r), (hop2_rows, z2_r)))]
    m1 = [remote(win.at[core, s, hop1_rows], win.at[core, s, hop1_rows], m1_s.at[s], m1_r.at[s], mate)
          for s in stages]
    m1_in = [remote(win.at[other, s, hop1_rows], win.at[other, s, hop1_rows], m1_s.at[s], m1_r.at[s], mate)
             for s in stages]
    m2 = [remote(win.at[core, s, hop2_rows], win.at[core, s, hop2_rows], m2_s.at[s], m2_r.at[s], mate)
          for s in stages]
    m2_in = [remote(win.at[other, s, hop2_rows], win.at[other, s, hop2_rows], m2_s.at[s], m2_r.at[s], mate)
             for s in stages]
    xq = [[remote(ref.at[:, :, cols(1 - chip, s)], qo.at[kind, s, :, 1], x_s.at[kind, s], x_r.at[kind, s], partner)
           for kind, ref in ((0, q_ref), (1, g_ref))] for s in stages]
    mate_rows = (hop2_rows, pl.ds(TOK, 2 * TOK))
    mt = [[remote(mate_out.at[s, mate_rows[h]], mate_in.at[s, mate_rows[h]], mt_s.at[s, h], mt_r.at[s, h], mate)
           for h in halves] for s in stages]
    quarters = [pl.ds(q * 128, 128) for q in range(4)]
    r2 = [[remote(r2_out.at[s, rows], r2_in.at[s, rows], r2_s.at[s, q], r2_r.at[s, q], prv)
           for q, rows in enumerate(quarters)] for s in stages]
    r1 = [[remote(r1_out.at[s, rows], r1_in.at[s, head], r1_s.at[s, q], r1_r.at[s, head], (prv[0], q))
           for q, rows in enumerate(quarters)] for s in stages]
    r1_from = [[remote(r1_out.at[s, quarters[0]], r1_in.at[s, h], r1_s.at[s, 0], r1_r.at[s, h], prv)
                for h in range(4)] for s in stages]
    h0 = [[remote(h0_out.at[s, rows], h0_in.at[s, head], h0_s.at[s, q], h0_r.at[s, head], (ctx, q))
           for q, rows in enumerate(quarters)] for s in stages]
    h0_from = [[remote(h0_out.at[s, quarters[0]], h0_in.at[s, h], h0_s.at[s, 0], h0_r.at[s, h], mate)
                for h in range(4)] for s in stages]
    dq_far = [remote(dqs.at[s, 1], dq_ref.at[:, :, cols(chip, s)], dq_s.at[s], dq_r.at[s], partner)
              for s in stages]
    dq_far_in = [remote(dqs.at[s, 1], dq_ref.at[:, :, cols(1 - chip, s)], dq_s.at[s], dq_r.at[s], partner)
                 for s in stages]
    dq_near = [pltpu.make_async_copy(dqs.at[s, 0], dq_ref.at[:, :, cols(chip, s)], dq_l.at[s])
               for s in stages]

    z1[0].start()

    def either(direct, relayed):
        @pl.when(at_end)
        def _():
            relayed.start()

        @pl.when(jnp.logical_not(at_end))
        def _():
            direct.start()

    either(z1[1], z1_relayed)
    for copy in xq[0]:
        copy.start()

    @pl.when(jnp.logical_not(at_start | at_end))
    def _():
        for copy in xq[1]:
            copy.start()


    lengths = len_ref[...]
    upto = jnp.where(
        lax.broadcasted_iota(jnp.int32, (64, HD), 0) <= lax.broadcasted_iota(jnp.int32, (64, HD), 1), 1.0, 0.0
    ).astype(jnp.bfloat16)

    def ends_of(part):
        rows = jnp.broadcast_to(part, (16, 64)).astype(jnp.float32).astype(jnp.bfloat16)
        return mm(rows, upto)[0:1]

    ends = (ends_of(lengths >> 5) * 32.0 + ends_of(lengths & 31)).astype(jnp.int32)
    wide = (16, 64)
    before = jnp.where(
        lax.broadcasted_iota(jnp.int32, (64, HD), 0) < lax.broadcasted_iota(jnp.int32, (64, HD), 1), 1.0, 0.0
    ).astype(jnp.bfloat16)

    def starts_of(part):
        rows = jnp.broadcast_to(part, wide).astype(jnp.float32).astype(jnp.bfloat16)
        return mm(rows, before)[0:1]

    starts = (starts_of(lengths >> 5) * 32.0 + starts_of(lengths & 31)).astype(jnp.int32)
    lane = lax.broadcasted_iota(jnp.int32, (1, HD), 1)
    starts = jnp.where(lane == 64, -WIN, starts)
    ends = jnp.where(lane == 64, 0, ends)

    def inside(count, base):
        pos = lax.broadcasted_iota(jnp.int32, (count, HD), 0) + base
        return (starts <= pos) & (pos < ends)

    for t in range(0, WIN, HALF):
        key_doc[t:t + HALF] = jnp.where(inside(HALF, ctx * TOK - REACH + t), 1.0, 0.0).astype(jnp.bfloat16)
    for t in range(0, TOK, HALF):
        query_doc[t:t + HALF] = jnp.where(inside(HALF, ctx * TOK + t), 0.0, -1e30).astype(jnp.bfloat16)

    causal = (lax.broadcasted_iota(jnp.int32, (HALF, HALF), 0)
              <= lax.broadcasted_iota(jnp.int32, (HALF, HALF), 1))

    def fold(x):
        return jnp.sum(x.reshape(x.shape[0] // 8, 8, x.shape[1]), axis=0)

    slots = {(0, 0): 0, (0, 1): 2, (1, 0): 4, (1, 1): 0}

    def part(s, c, j, low, high):
        slot = slots[s, j] + c
        score, wgrad = scores.at[slot], wgrads.at[slot]
        rows = pl.ds(c * HALF + low, high - low)
        keyed = jnp.concatenate([win[0, s, rows], key_doc[rows]], axis=1)
        asked = jnp.concatenate([qo[0, s, c, j], query_doc[c * HALF:(c + 1) * HALF]], axis=1)
        score[low:high] = lax.dot_general(keyed, asked, NT, preferred_element_type=jnp.float32)
        wgrad[low:high] = lax.dot_general(
            win[1, s, rows], qo[1, s, c, j], NT, preferred_element_type=jnp.float32)
        if high == SPAN:
            score[REACH:SPAN] = jnp.where(causal, score[REACH:SPAN], -1e30)
        peak = None
        for t in range(low, high, TILE):
            x = score[t:t + TILE]
            x = jnp.max(x.reshape(TILE // 8, 8, HALF), axis=0)
            peak = x if peak is None else jnp.maximum(peak, x)
        top = jnp.max(peak, axis=0, keepdims=True)
        total = jnp.zeros((8, HALF), jnp.float32)
        dots = jnp.zeros((8, HALF), jnp.float32)
        for t in range(low, high, TILE):
            e = jnp.exp2((score[t:t + TILE] - top) * (SCALE * LOG2E))
            score[t:t + TILE] = e
            total += fold(e)
            dots += fold(e * wgrad[t:t + TILE])
        return top, jnp.sum(total, axis=0, keepdims=True), jnp.sum(dots, axis=0, keepdims=True)

    def early(s, c, j):
        slot = slots[s, j] + c
        for row, value in enumerate(part(s, c, j, TOK - c * HALF, SPAN)):
            stats[slot, row:row + 1] = value

    def late(s, c, j):
        slot, border = slots[s, j] + c, TOK - c * HALF
        score, wgrad = scores.at[slot], wgrads.at[slot]
        far_top, far_total, far_dots = part(s, c, j, 0, border)
        near_top, near_total, near_dots = (stats[slot, row:row + 1] for row in range(3))
        top = jnp.maximum(far_top, near_top)
        far_scale = jnp.exp2((far_top - top) * (SCALE * LOG2E))
        near_scale = jnp.exp2((near_top - top) * (SCALE * LOG2E))
        inverse = 1.0 / (far_total * far_scale + near_total * near_scale)
        delta = (far_dots * far_scale + near_dots * near_scale) * inverse
        at = pl.ds(c * TOK + j * HALF, HALF)
        for t in range(0, SPAN, TILE):
            weights = score[t:t + TILE] * ((far_scale if t < border else near_scale) * inverse)
            rows = slice(c * HALF + t, c * HALF + t + TILE)
            pd[s, 1, rows, at] = weights.astype(jnp.bfloat16)
            pd[s, 0, rows, at] = (weights * (wgrad[t:t + TILE] - delta)).astype(jnp.bfloat16)

    def query_grads(s):
        for c in halves:
            rows = pl.ds(c * HALF, SPAN)
            found = lax.dot_general(
                pd[s, 0, rows, c * TOK:(c + 1) * TOK], win[0, s, rows], TN, preferred_element_type=jnp.float32)
            dqs[s, :, c] = (found * SCALE).astype(jnp.bfloat16).reshape(2, HALF, HD)
        dq_far[s].start()
        dq_near[s].start()

    pieces = (((0, HALF, 0, 1), (HALF, TOK, 0, 2)), ((TOK, SPAN, 0, 2), (SPAN, WIN, 1, 2)))

    def product(kind, s, piece):
        low, high, c0, c1 = piece
        right = qo[kind, s, c0:c1].reshape(((c1 - c0) * TOK, HD))
        return mm(pd[s, kind, low:high, c0 * TOK:c1 * TOK], right) * jnp.where(kind == 0, SCALE, 1.0)

    def theirs(s, h):
        for piece in pieces[h]:
            mate_out[s, piece[0]:piece[1]] = product(other, s, piece).astype(jnp.bfloat16)
        mt[s][h].start()

    def ours(s, h):
        for piece in pieces[h]:
            mine[piece[0]:piece[1]] = product(core, s, piece)

    def outer(s):
        theirs(s, 0)
        ours(s, 0)
        theirs(s, 1)
        mt[s][0].wait_recv()
        for q in range(4):
            at = slice(q * 128, (q + 1) * 128)
            r2_out[s, at] = (mine[at] + mate_in[s, at].astype(jnp.float32)).astype(jnp.bfloat16)
            r2[s][q].start()
        ours(s, 1)
        mt[s][1].wait_recv()
        hop1[s] = mine[TOK:REACH] + mate_in[s, TOK:REACH].astype(jnp.float32)
        h0_out[s] = (mine[REACH:WIN] + mate_in[s, REACH:WIN].astype(jnp.float32)).astype(jnp.bfloat16)
        for q in range(4):
            @pl.when(head != q)
            def _(q=q):
                h0[s][q].start()

            @pl.when(head == q)
            def _(q=q):
                pltpu.make_async_copy(h0_out.at[s, quarters[q]], h0_in.at[s, q], h0_r.at[s, q]).start()

    def middle(s):
        for q in range(4):
            at = slice(q * 128, (q + 1) * 128)
            r2[s][q].wait_recv()
            r1_out[s, at] = (hop1[s, at] + r2_in[s, at].astype(jnp.float32)).astype(jnp.bfloat16)
            r1[s][q].start()

    def finish(s):
        for h in range(4):
            h0_from[s][h].wait_recv()
            r1_from[s][h].wait_recv()
            out = (dk_ref, dv_ref)[h % 2]
            g = (h // 2) * 2 + s
            out[:, g * HD:(g + 1) * HD] = (
                h0_in[s, h].astype(jnp.float32) + r1_in[s, h].astype(jnp.float32)).astype(jnp.bfloat16)

    def forward(s):
        z1[s].wait_recv()
        if s == 1:
            either(z2[1], z2_relayed)
        else:
            z2[s].start()
        m1[s].start()

    def pass_on(k):
        @pl.when(at_end)
        def _():
            (z1_relayed, z2_relayed)[k].wait_recv()
            passed[k].start()

    def arrive(s):
        z2[s].wait_recv()
        m2[s].start()

    forward(0)
    m1_in[0].wait_recv()
    early(0, 0, 0)
    early(0, 1, 0)

    @pl.when(jnp.logical_not(at_start))
    def _():
        forward(1)

    pass_on(0)

    @pl.when(jnp.logical_not(at_start))
    def _():
        m1_in[1].wait_recv()
        early(1, 0, 0)
        early(1, 1, 0)

    for copy in xq[0]:
        copy.wait_recv()

    @pl.when(at_start | at_end)
    def _():
        for copy in xq[1]:
            copy.start()

    early(0, 0, 1)
    arrive(0)
    early(0, 1, 1)
    m2_in[0].wait_recv()
    late(0, 0, 0)

    @pl.when(at_start)
    def _():
        forward(1)

    late(0, 1, 0)
    pass_on(1)
    late(0, 0, 1)
    late(0, 1, 1)
    outer(0)

    @pl.when(at_start)
    def _():
        m1_in[1].wait_recv()
        early(1, 0, 0)
        early(1, 1, 0)

    arrive(1)
    query_grads(0)
    m2_in[1].wait_recv()
    late(1, 0, 0)
    late(1, 1, 0)
    middle(0)
    for copy in xq[1]:
        copy.wait_recv()
    early(1, 0, 1)
    late(1, 0, 1)
    early(1, 1, 1)
    late(1, 1, 1)
    outer(1)
    query_grads(1)
    middle(1)
    finish(0)
    finish(1)

    @pl.when(at_end)
    def _():
        for copy in passed:
            copy.wait_send()

    for s in stages:
        for copy in (z1[s], z2[s], m1[s], m2[s], *xq[s], *mt[s], *r2[s], *r1[s], dq_far[s]):
            copy.wait_send()
        for q in range(4):
            @pl.when(head != q)
            def _(q=q):
                h0[s][q].wait_send()
        dq_far_in[s].wait_recv()
        dq_near[s].wait()


def write_out(*refs):
    sources, targets, sem = refs[0:3], refs[3:6], refs[6]
    copies = [pltpu.make_async_copy(source, target, sem.at[i])
              for i, (source, target) in enumerate(zip(sources, targets, strict=True))]
    for copy in copies:
        copy.start()
    for copy in copies:
        copy.wait()


def local(ctx_size, queries, keys, values, grad_out, doc_lengths):
    bf16, f32 = jnp.bfloat16, jnp.float32
    anywhere = pl.BlockSpec(memory_space=pl.ANY)
    pair = pltpu.SemaphoreType.DMA((STAGES,))
    quad = pltpu.SemaphoreType.DMA((STAGES, 2))
    eight = pltpu.SemaphoreType.DMA((STAGES, 4))
    block16 = pltpu.VMEM((STAGES, TOK, HD), bf16)
    heads16 = pltpu.VMEM((STAGES, 4, 128, HD), bf16)
    dq, dk, dv = pl.pallas_call(
        lambda *refs: kernel(ctx_size, *refs),
        out_shape=(
            pltpu.VMEM((2, HALF, KVH * HD), bf16),
            pltpu.VMEM((128, KVH * HD), bf16),
            pltpu.VMEM((128, KVH * HD), bf16),
        ),
        in_specs=[anywhere] * 4 + [pl.BlockSpec(memory_space=pltpu.VMEM)],
        out_specs=(pl.BlockSpec(memory_space=pltpu.VMEM), pl.BlockSpec(memory_space=pltpu.VMEM), pl.BlockSpec(memory_space=pltpu.VMEM)),
        scratch_shapes=[
            pltpu.VMEM((2, STAGES, WIN, HD), bf16),
            pltpu.VMEM((2, STAGES, 2, 2, HALF, HD), bf16),
            pltpu.VMEM((STAGES, 2, WIN, 2 * TOK), bf16),
            pltpu.VMEM((6, SPAN, HALF), f32),
            pltpu.VMEM((6, SPAN, HALF), f32),
            pltpu.VMEM((6, 8, HALF), f32),
            pltpu.VMEM((WIN, HD), f32),
            pltpu.VMEM((STAGES, 2, 2, HALF, HD), bf16),
            pltpu.VMEM((WIN, HD), bf16),
            pltpu.VMEM((TOK, HD), bf16),
            pltpu.VMEM((STAGES, WIN, HD), bf16),
            pltpu.VMEM((STAGES, WIN, HD), bf16),
            pltpu.VMEM((STAGES, TOK, HD), f32),
            block16, block16, block16, heads16, block16, heads16,
            block16,
            pltpu.SemaphoreType.DMA((4, STAGES)),
            pair, pair, pair, pair, pair, pair, pair, pair,
            quad, quad,
            quad, quad, eight, eight, eight, eight, pair, pair, pair,
            eight, eight,
            pair, pair,
        ],
        compiler_params=pltpu.CompilerParams(
            collective_id=0, has_side_effects=True, vmem_limit_bytes=56 * 2**20),
        cost_estimate=pl.CostEstimate(
            flops=10 * 4 * TOK * SPAN * HD, bytes_accessed=4 * 2**20, transcendentals=4 * TOK * SPAN),
        name="attention_backward",
    )(queries.reshape(2, HALF, KVH * HD), keys, values, grad_out.reshape(2, HALF, KVH * HD),
      doc_lengths.reshape(1, 64))
    dq, dk, dv = pl.pallas_call(
        write_out,
        out_shape=tuple(jax.ShapeDtypeStruct(x.shape, bf16) for x in (dq, dk, dv)),
        in_specs=[anywhere] * 3,
        out_specs=(anywhere,) * 3,
        scratch_shapes=[pltpu.SemaphoreType.DMA((3,))],
        compiler_params=pltpu.CompilerParams(vmem_limit_bytes=4 * 2**20),
        name="write_out",
    )(dq, dk, dv)
    return dq.reshape(TOK, 1, KVH * HD), dk, dv


def solution(mesh):
    placed = (P("ctx", "head", None), P("ctx", None), P("ctx", None), P("ctx", "head", None), P())
    ctx_size = mesh.shape["ctx"]
    return jax.shard_map(
        lambda *args: local(ctx_size, *args),
        mesh=mesh,
        in_specs=placed,
        out_specs=(P("ctx", "head", None), P(("ctx", "head"), None), P(("ctx", "head"), None)),
        check_vma=False,
    )
```

```python
import math

import jax
import jax.numpy as jnp
from jax import lax
from jax.experimental import pallas as pl
from jax.experimental.pallas import tpu as pltpu
from jax.sharding import PartitionSpec as P

HD = 128
KVH = 4
TOK = 512
HALF = 256
REACH = 1024
WIN = REACH + TOK
SPAN = REACH + HALF
TILE = 64
STAGES = 2
ROW = 8
MESH = pl.DeviceIdType.MESH
SCALE = 1.0 / math.sqrt(HD)
LOG2E = math.log2(math.e)
NT = (((1,), (1,)), ((), ()))
TN = (((0,), (0,)), ((), ()))


def mm(a, b):
    return jnp.dot(a, b, preferred_element_type=jnp.float32)


def kernel(
    ctx_size,
    q_ref, k_ref, v_ref, g_ref, len_ref,
    dq_ref, dk_ref, dv_ref,
    win, qo, pd, scores, wgrads, stats, mine, dqs, key_doc, query_doc,
    mate_out, mate_in, hop1, r2_out, r2_in, r1_out, r1_in, h0_out, h0_in, relay,
    load_sem, z1_s, z1_r, z2_s, z2_r, m1_s, m1_r, m2_s, m2_r, x_s, x_r,
    mt_s, mt_r, r2_s, r2_r, r1_s, r1_r, dq_s, dq_r, dq_l, h0_s, h0_r, relay_s, relay_r,
):
    ctx = lax.axis_index("ctx")
    head = lax.axis_index("head")
    core = lax.rem(head, 2)
    chip = head // 2
    other = 1 - core
    nxt = (lax.rem(ctx + 1, ctx_size), head)
    prv = (lax.rem(ctx + ctx_size - 1, ctx_size), head)
    mate = (ctx, chip * 2 + other)
    partner = (ctx, (1 - chip) * 2 + core)
    diagonal = (ctx, (1 - chip) * 2 + other)
    stages, halves = range(STAGES), range(2)
    place = lax.rem(ctx, ROW)
    at_start, at_end = place == 0, place == ROW - 1

    def near(steps):
        return (lax.rem(ctx + ctx_size + steps, ctx_size), head)

    relay_to, relay_from, relay_down, relay_up = near(ROW), near(-ROW), near(1 - ROW), near(ROW - 1)

    def cols(owner, s):
        return pl.ds(pl.multiple_of((owner * 2 + s) * HD, HD), HD)

    def remote(src, dst, send, recv, device):
        return pltpu.make_async_remote_copy(
            src_ref=src, dst_ref=dst, send_sem=send, recv_sem=recv,
            device_id=device, device_id_type=MESH,
        )

    own_rows = pl.ds(REACH, TOK)
    hop1_rows = pl.ds(TOK, TOK)
    hop2_rows = pl.ds(0, TOK)

    loads = []
    for s in stages:
        for kind, ref in ((0, k_ref), (1, v_ref)):
            loads.append(pltpu.make_async_copy(
                ref.at[:, cols(chip, s)], win.at[kind, s, own_rows], load_sem.at[kind, s]))
        for kind, ref in ((0, q_ref), (1, g_ref)):
            loads.append(pltpu.make_async_copy(
                ref.at[:, :, cols(chip, s)], qo.at[kind, s, :, 0], load_sem.at[2 + kind, s]))
    for load in loads:
        load.start()

    barrier = pltpu.get_barrier_semaphore()
    for device in (mate, partner, diagonal, *[(nxt[0], h) for h in range(4)], *[(prv[0], h) for h in range(4)]):
        pl.semaphore_signal(barrier, 1, device_id=device, device_id_type=MESH)

    @pl.when(at_end)
    def _():
        for device in (relay_to, relay_from, relay_down):
            pl.semaphore_signal(barrier, 1, device_id=device, device_id_type=MESH)

    @pl.when(at_start)
    def _():
        pl.semaphore_signal(barrier, 1, device_id=relay_up, device_id_type=MESH)

    for load in loads:
        load.wait()
    pl.semaphore_wait(barrier, 11 + 3 * (place // (ROW - 1)) + (ROW - 1 - place) // (ROW - 1))

    z1 = [remote(win.at[core, s, own_rows], win.at[core, s, hop1_rows], z1_s.at[s], z1_r.at[s], nxt) for s in stages]
    z2 = [remote(win.at[core, s, hop1_rows], win.at[core, s, hop2_rows], z2_s.at[s], z2_r.at[s], nxt) for s in stages]
    z1_relayed = remote(win.at[core, 1, own_rows], relay.at[0], z1_s.at[1], relay_r.at[0], relay_to)
    z2_relayed = remote(win.at[core, 1, hop1_rows], relay.at[1], z2_s.at[1], relay_r.at[1], relay_to)
    passed = [remote(relay.at[k], win.at[core, 1, rows], relay_s.at[k], sem.at[1], relay_down)
              for k, (rows, sem) in enumerate(((hop1_rows, z1_r), (hop2_rows, z2_r)))]
    m1 = [remote(win.at[core, s, hop1_rows], win.at[core, s, hop1_rows], m1_s.at[s], m1_r.at[s], mate)
          for s in stages]
    m1_in = [remote(win.at[other, s, hop1_rows], win.at[other, s, hop1_rows], m1_s.at[s], m1_r.at[s], mate)
             for s in stages]
    m2 = [remote(win.at[core, s, hop2_rows], win.at[core, s, hop2_rows], m2_s.at[s], m2_r.at[s], mate)
          for s in stages]
    m2_in = [remote(win.at[other, s, hop2_rows], win.at[other, s, hop2_rows], m2_s.at[s], m2_r.at[s], mate)
             for s in stages]
    xq = [[remote(ref.at[:, :, cols(1 - chip, s)], qo.at[kind, s, :, 1], x_s.at[kind, s], x_r.at[kind, s], partner)
           for kind, ref in ((0, q_ref), (1, g_ref))] for s in stages]
    mate_rows = (hop2_rows, pl.ds(TOK, 2 * TOK))
    mt = [[remote(mate_out.at[s, mate_rows[h]], mate_in.at[s, mate_rows[h]], mt_s.at[s, h], mt_r.at[s, h], mate)
           for h in halves] for s in stages]
    quarters = [pl.ds(q * 128, 128) for q in range(4)]
    r2 = [[remote(r2_out.at[s, rows], r2_in.at[s, rows], r2_s.at[s, q], r2_r.at[s, q], prv)
           for q, rows in enumerate(quarters)] for s in stages]
    r1 = [[remote(r1_out.at[s, rows], r1_in.at[s, head], r1_s.at[s, q], r1_r.at[s, head], (prv[0], q))
           for q, rows in enumerate(quarters)] for s in stages]
    r1_from = [[remote(r1_out.at[s, quarters[0]], r1_in.at[s, h], r1_s.at[s, 0], r1_r.at[s, h], prv)
                for h in range(4)] for s in stages]
    h0 = [[remote(h0_out.at[s, rows], h0_in.at[s, head], h0_s.at[s, q], h0_r.at[s, head], (ctx, q))
           for q, rows in enumerate(quarters)] for s in stages]
    h0_from = [[remote(h0_out.at[s, quarters[0]], h0_in.at[s, h], h0_s.at[s, 0], h0_r.at[s, h], mate)
                for h in range(4)] for s in stages]
    dq_far = [remote(dqs.at[s, 1], dq_ref.at[:, :, cols(chip, s)], dq_s.at[s], dq_r.at[s], partner)
              for s in stages]
    dq_far_in = [remote(dqs.at[s, 1], dq_ref.at[:, :, cols(1 - chip, s)], dq_s.at[s], dq_r.at[s], partner)
                 for s in stages]
    dq_near = [pltpu.make_async_copy(dqs.at[s, 0], dq_ref.at[:, :, cols(chip, s)], dq_l.at[s])
               for s in stages]

    z1[0].start()

    def either(direct, relayed):
        @pl.when(at_end)
        def _():
            relayed.start()

        @pl.when(jnp.logical_not(at_end))
        def _():
            direct.start()

    either(z1[1], z1_relayed)
    for copy in xq[0]:
        copy.start()

    @pl.when(jnp.logical_not(at_start | at_end))
    def _():
        for copy in xq[1]:
            copy.start()


    lengths = len_ref[...]
    upto = jnp.where(
        lax.broadcasted_iota(jnp.int32, (64, HD), 0) <= lax.broadcasted_iota(jnp.int32, (64, HD), 1), 1.0, 0.0
    ).astype(jnp.bfloat16)

    def ends_of(part):
        rows = jnp.broadcast_to(part, (16, 64)).astype(jnp.float32).astype(jnp.bfloat16)
        return mm(rows, upto)[0:1]

    ends = (ends_of(lengths >> 5) * 32.0 + ends_of(lengths & 31)).astype(jnp.int32)
    wide = (16, 64)
    before = jnp.where(
        lax.broadcasted_iota(jnp.int32, (64, HD), 0) < lax.broadcasted_iota(jnp.int32, (64, HD), 1), 1.0, 0.0
    ).astype(jnp.bfloat16)

    def starts_of(part):
        rows = jnp.broadcast_to(part, wide).astype(jnp.float32).astype(jnp.bfloat16)
        return mm(rows, before)[0:1]

    starts = (starts_of(lengths >> 5) * 32.0 + starts_of(lengths & 31)).astype(jnp.int32)
    lane = lax.broadcasted_iota(jnp.int32, (1, HD), 1)
    starts = jnp.where(lane == 64, -WIN, starts)
    ends = jnp.where(lane == 64, 0, ends)

    def inside(count, base):
        pos = lax.broadcasted_iota(jnp.int32, (count, HD), 0) + base
        return (starts <= pos) & (pos < ends)

    for t in range(0, WIN, HALF):
        key_doc[t:t + HALF] = jnp.where(inside(HALF, ctx * TOK - REACH + t), 1.0, 0.0).astype(jnp.bfloat16)
    for t in range(0, TOK, HALF):
        query_doc[t:t + HALF] = jnp.where(inside(HALF, ctx * TOK + t), 0.0, -1e30).astype(jnp.bfloat16)

    causal = (lax.broadcasted_iota(jnp.int32, (HALF, HALF), 0)
              <= lax.broadcasted_iota(jnp.int32, (HALF, HALF), 1))

    def fold(x):
        return jnp.sum(x.reshape(x.shape[0] // 8, 8, x.shape[1]), axis=0)

    slots = {(0, 0): 0, (0, 1): 2, (1, 0): 4, (1, 1): 0}

    def part(s, c, j, low, high):
        slot = slots[s, j] + c
        score, wgrad = scores.at[slot], wgrads.at[slot]
        rows = pl.ds(c * HALF + low, high - low)
        keyed = jnp.concatenate([win[0, s, rows], key_doc[rows]], axis=1)
        asked = jnp.concatenate([qo[0, s, c, j], query_doc[c * HALF:(c + 1) * HALF]], axis=1)
        score[low:high] = lax.dot_general(keyed, asked, NT, preferred_element_type=jnp.float32)
        wgrad[low:high] = lax.dot_general(
            win[1, s, rows], qo[1, s, c, j], NT, preferred_element_type=jnp.float32)
        if high == SPAN:
            score[REACH:SPAN] = jnp.where(causal, score[REACH:SPAN], -1e30)
        peak = None
        for t in range(low, high, TILE):
            x = score[t:t + TILE]
            x = jnp.max(x.reshape(TILE // 8, 8, HALF), axis=0)
            peak = x if peak is None else jnp.maximum(peak, x)
        top = jnp.max(peak, axis=0, keepdims=True)
        total = jnp.zeros((8, HALF), jnp.float32)
        dots = jnp.zeros((8, HALF), jnp.float32)
        for t in range(low, high, TILE):
            e = jnp.exp2((score[t:t + TILE] - top) * (SCALE * LOG2E))
            score[t:t + TILE] = e
            total += fold(e)
            dots += fold(e * wgrad[t:t + TILE])
        return top, jnp.sum(total, axis=0, keepdims=True), jnp.sum(dots, axis=0, keepdims=True)

    def early(s, c, j):
        slot = slots[s, j] + c
        for row, value in enumerate(part(s, c, j, TOK - c * HALF, SPAN)):
            stats[slot, row:row + 1] = value

    def late(s, c, j):
        slot, border = slots[s, j] + c, TOK - c * HALF
        score, wgrad = scores.at[slot], wgrads.at[slot]
        far_top, far_total, far_dots = part(s, c, j, 0, border)
        near_top, near_total, near_dots = (stats[slot, row:row + 1] for row in range(3))
        top = jnp.maximum(far_top, near_top)
        far_scale = jnp.exp2((far_top - top) * (SCALE * LOG2E))
        near_scale = jnp.exp2((near_top - top) * (SCALE * LOG2E))
        inverse = 1.0 / (far_total * far_scale + near_total * near_scale)
        delta = (far_dots * far_scale + near_dots * near_scale) * inverse
        at = pl.ds(c * TOK + j * HALF, HALF)
        for t in range(0, SPAN, TILE):
            weights = score[t:t + TILE] * ((far_scale if t < border else near_scale) * inverse)
            rows = slice(c * HALF + t, c * HALF + t + TILE)
            pd[s, 1, rows, at] = weights.astype(jnp.bfloat16)
            pd[s, 0, rows, at] = (weights * (wgrad[t:t + TILE] - delta)).astype(jnp.bfloat16)

    def query_grads(s):
        for c in halves:
            rows = pl.ds(c * HALF, SPAN)
            found = lax.dot_general(
                pd[s, 0, rows, c * TOK:(c + 1) * TOK], win[0, s, rows], TN, preferred_element_type=jnp.float32)
            dqs[s, :, c] = (found * SCALE).astype(jnp.bfloat16).reshape(2, HALF, HD)
        dq_far[s].start()
        dq_near[s].start()

    pieces = (((0, HALF, 0, 1), (HALF, TOK, 0, 2)), ((TOK, SPAN, 0, 2), (SPAN, WIN, 1, 2)))

    def product(kind, s, piece):
        low, high, c0, c1 = piece
        right = qo[kind, s, c0:c1].reshape(((c1 - c0) * TOK, HD))
        return mm(pd[s, kind, low:high, c0 * TOK:c1 * TOK], right) * jnp.where(kind == 0, SCALE, 1.0)

    def theirs(s, h):
        for piece in pieces[h]:
            mate_out[s, piece[0]:piece[1]] = product(other, s, piece).astype(jnp.bfloat16)
        mt[s][h].start()

    def ours(s, h):
        for piece in pieces[h]:
            mine[piece[0]:piece[1]] = product(core, s, piece)

    def outer(s):
        theirs(s, 0)
        ours(s, 0)
        theirs(s, 1)
        mt[s][0].wait_recv()
        for q in range(4):
            at = slice(q * 128, (q + 1) * 128)
            r2_out[s, at] = (mine[at] + mate_in[s, at].astype(jnp.float32)).astype(jnp.bfloat16)
            r2[s][q].start()
        ours(s, 1)
        mt[s][1].wait_recv()
        hop1[s] = mine[TOK:REACH] + mate_in[s, TOK:REACH].astype(jnp.float32)
        h0_out[s] = (mine[REACH:WIN] + mate_in[s, REACH:WIN].astype(jnp.float32)).astype(jnp.bfloat16)
        for q in range(4):
            @pl.when(head != q)
            def _(q=q):
                h0[s][q].start()

            @pl.when(head == q)
            def _(q=q):
                pltpu.make_async_copy(h0_out.at[s, quarters[q]], h0_in.at[s, q], h0_r.at[s, q]).start()

    def middle(s):
        for q in range(4):
            at = slice(q * 128, (q + 1) * 128)
            r2[s][q].wait_recv()
            r1_out[s, at] = (hop1[s, at] + r2_in[s, at].astype(jnp.float32)).astype(jnp.bfloat16)
            r1[s][q].start()

    def finish(s):
        for h in range(4):
            h0_from[s][h].wait_recv()
            r1_from[s][h].wait_recv()
            out = (dk_ref, dv_ref)[h % 2]
            g = (h // 2) * 2 + s
            out[:, g * HD:(g + 1) * HD] = (
                h0_in[s, h].astype(jnp.float32) + r1_in[s, h].astype(jnp.float32)).astype(jnp.bfloat16)

    def forward(s):
        z1[s].wait_recv()
        if s == 1:
            either(z2[1], z2_relayed)
        else:
            z2[s].start()
        m1[s].start()

    def pass_on(k):
        @pl.when(at_end)
        def _():
            (z1_relayed, z2_relayed)[k].wait_recv()
            passed[k].start()

    def arrive(s):
        z2[s].wait_recv()
        m2[s].start()

    forward(0)
    m1_in[0].wait_recv()
    early(0, 0, 0)
    early(0, 1, 0)

    @pl.when(jnp.logical_not(at_start))
    def _():
        forward(1)

    pass_on(0)

    @pl.when(jnp.logical_not(at_start))
    def _():
        m1_in[1].wait_recv()
        early(1, 0, 0)
        early(1, 1, 0)

    for copy in xq[0]:
        copy.wait_recv()

    @pl.when(at_start | at_end)
    def _():
        for copy in xq[1]:
            copy.start()

    early(0, 0, 1)
    arrive(0)
    early(0, 1, 1)
    m2_in[0].wait_recv()
    late(0, 0, 0)

    @pl.when(at_start)
    def _():
        forward(1)

    pass_on(1)
    late(0, 1, 0)
    late(0, 0, 1)
    late(0, 1, 1)
    outer(0)

    @pl.when(at_start)
    def _():
        m1_in[1].wait_recv()
        early(1, 0, 0)
        early(1, 1, 0)

    arrive(1)
    query_grads(0)
    m2_in[1].wait_recv()
    late(1, 0, 0)
    late(1, 1, 0)
    middle(0)
    for copy in xq[1]:
        copy.wait_recv()
    early(1, 0, 1)
    late(1, 0, 1)
    early(1, 1, 1)
    late(1, 1, 1)
    outer(1)
    query_grads(1)
    middle(1)
    finish(0)
    finish(1)

    @pl.when(at_end)
    def _():
        for copy in passed:
            copy.wait_send()

    for s in stages:
        for copy in (z1[s], z2[s], m1[s], m2[s], *xq[s], *mt[s], *r2[s], *r1[s], dq_far[s]):
            copy.wait_send()
        for q in range(4):
            @pl.when(head != q)
            def _(q=q):
                h0[s][q].wait_send()
        dq_far_in[s].wait_recv()
        dq_near[s].wait()


def write_out(*refs):
    sources, targets, sem = refs[0:3], refs[3:6], refs[6]
    copies = [pltpu.make_async_copy(source, target, sem.at[i])
              for i, (source, target) in enumerate(zip(sources, targets, strict=True))]
    for copy in copies:
        copy.start()
    for copy in copies:
        copy.wait()


def local(ctx_size, queries, keys, values, grad_out, doc_lengths):
    bf16, f32 = jnp.bfloat16, jnp.float32
    anywhere = pl.BlockSpec(memory_space=pl.ANY)
    pair = pltpu.SemaphoreType.DMA((STAGES,))
    quad = pltpu.SemaphoreType.DMA((STAGES, 2))
    eight = pltpu.SemaphoreType.DMA((STAGES, 4))
    block16 = pltpu.VMEM((STAGES, TOK, HD), bf16)
    heads16 = pltpu.VMEM((STAGES, 4, 128, HD), bf16)
    dq, dk, dv = pl.pallas_call(
        lambda *refs: kernel(ctx_size, *refs),
        out_shape=(
            pltpu.VMEM((2, HALF, KVH * HD), bf16),
            pltpu.VMEM((128, KVH * HD), bf16),
            pltpu.VMEM((128, KVH * HD), bf16),
        ),
        in_specs=[anywhere] * 4 + [pl.BlockSpec(memory_space=pltpu.VMEM)],
        out_specs=(pl.BlockSpec(memory_space=pltpu.VMEM), pl.BlockSpec(memory_space=pltpu.VMEM), pl.BlockSpec(memory_space=pltpu.VMEM)),
        scratch_shapes=[
            pltpu.VMEM((2, STAGES, WIN, HD), bf16),
            pltpu.VMEM((2, STAGES, 2, 2, HALF, HD), bf16),
            pltpu.VMEM((STAGES, 2, WIN, 2 * TOK), bf16),
            pltpu.VMEM((6, SPAN, HALF), f32),
            pltpu.VMEM((6, SPAN, HALF), f32),
            pltpu.VMEM((6, 8, HALF), f32),
            pltpu.VMEM((WIN, HD), f32),
            pltpu.VMEM((STAGES, 2, 2, HALF, HD), bf16),
            pltpu.VMEM((WIN, HD), bf16),
            pltpu.VMEM((TOK, HD), bf16),
            pltpu.VMEM((STAGES, WIN, HD), bf16),
            pltpu.VMEM((STAGES, WIN, HD), bf16),
            pltpu.VMEM((STAGES, TOK, HD), f32),
            block16, block16, block16, heads16, block16, heads16,
            block16,
            pltpu.SemaphoreType.DMA((4, STAGES)),
            pair, pair, pair, pair, pair, pair, pair, pair,
            quad, quad,
            quad, quad, eight, eight, eight, eight, pair, pair, pair,
            eight, eight,
            pair, pair,
        ],
        compiler_params=pltpu.CompilerParams(
            collective_id=0, has_side_effects=True, vmem_limit_bytes=56 * 2**20),
        cost_estimate=pl.CostEstimate(
            flops=10 * 4 * TOK * SPAN * HD, bytes_accessed=4 * 2**20, transcendentals=4 * TOK * SPAN),
        name="attention_backward",
    )(queries.reshape(2, HALF, KVH * HD), keys, values, grad_out.reshape(2, HALF, KVH * HD),
      doc_lengths.reshape(1, 64))
    dq, dk, dv = pl.pallas_call(
        write_out,
        out_shape=tuple(jax.ShapeDtypeStruct(x.shape, bf16) for x in (dq, dk, dv)),
        in_specs=[anywhere] * 3,
        out_specs=(anywhere,) * 3,
        scratch_shapes=[pltpu.SemaphoreType.DMA((3,))],
        compiler_params=pltpu.CompilerParams(vmem_limit_bytes=4 * 2**20),
        name="write_out",
    )(dq, dk, dv)
    return dq.reshape(TOK, 1, KVH * HD), dk, dv


def solution(mesh):
    placed = (P("ctx", "head", None), P("ctx", None), P("ctx", None), P("ctx", "head", None), P())
    ctx_size = mesh.shape["ctx"]
    return jax.shard_map(
        lambda *args: local(ctx_size, *args),
        mesh=mesh,
        in_specs=placed,
        out_specs=(P("ctx", "head", None), P(("ctx", "head"), None), P(("ctx", "head"), None)),
        check_vma=False,
    )
```

```python
import math

import jax
import jax.numpy as jnp
from jax import lax
from jax.experimental import pallas as pl
from jax.experimental.pallas import tpu as pltpu
from jax.sharding import PartitionSpec as P

HD = 128
KVH = 4
TOK = 512
HALF = 256
REACH = 1024
WIN = REACH + TOK
SPAN = REACH + HALF
TILE = 64
STAGES = 2
ROW = 8
MESH = pl.DeviceIdType.MESH
SCALE = 1.0 / math.sqrt(HD)
LOG2E = math.log2(math.e)
NT = (((1,), (1,)), ((), ()))
TN = (((0,), (0,)), ((), ()))


def mm(a, b):
    return jnp.dot(a, b, preferred_element_type=jnp.float32)


def kernel(
    ctx_size,
    q_ref, k_ref, v_ref, g_ref, len_ref,
    dq_ref, dk_ref, dv_ref,
    win, qo, pd, scores, wgrads, stats, mine, dqs, key_doc, query_doc,
    mate_out, mate_in, hop1, r2_out, r2_in, r1_out, r1_in, h0_out, h0_in, relay,
    load_sem, z1_s, z1_r, z2_s, z2_r, m1_s, m1_r, m2_s, m2_r, x_s, x_r,
    mt_s, mt_r, r2_s, r2_r, r1_s, r1_r, dq_s, dq_r, dq_l, h0_s, h0_r, relay_s, relay_r,
):
    ctx = lax.axis_index("ctx")
    head = lax.axis_index("head")
    core = lax.rem(head, 2)
    chip = head // 2
    other = 1 - core
    nxt = (lax.rem(ctx + 1, ctx_size), head)
    prv = (lax.rem(ctx + ctx_size - 1, ctx_size), head)
    mate = (ctx, chip * 2 + other)
    partner = (ctx, (1 - chip) * 2 + core)
    diagonal = (ctx, (1 - chip) * 2 + other)
    stages, halves = range(STAGES), range(2)
    place = lax.rem(ctx, ROW)
    at_start, at_end = place == 0, place == ROW - 1

    def near(steps):
        return (lax.rem(ctx + ctx_size + steps, ctx_size), head)

    relay_to, relay_from, relay_down, relay_up = near(ROW), near(-ROW), near(1 - ROW), near(ROW - 1)

    def cols(owner, s):
        return pl.ds(pl.multiple_of((owner * 2 + s) * HD, HD), HD)

    def remote(src, dst, send, recv, device):
        return pltpu.make_async_remote_copy(
            src_ref=src, dst_ref=dst, send_sem=send, recv_sem=recv,
            device_id=device, device_id_type=MESH,
        )

    own_rows = pl.ds(REACH, TOK)
    hop1_rows = pl.ds(TOK, TOK)
    hop2_rows = pl.ds(0, TOK)

    loads = []
    for s in stages:
        for kind, ref in ((0, k_ref), (1, v_ref)):
            loads.append(pltpu.make_async_copy(
                ref.at[:, cols(chip, s)], win.at[kind, s, own_rows], load_sem.at[kind, s]))
        for kind, ref in ((0, q_ref), (1, g_ref)):
            loads.append(pltpu.make_async_copy(
                ref.at[:, :, cols(chip, s)], qo.at[kind, s, :, 0], load_sem.at[2 + kind, s]))
    for load in loads:
        load.start()

    barrier = pltpu.get_barrier_semaphore()
    for device in (mate, partner, diagonal, *[(nxt[0], h) for h in range(4)], *[(prv[0], h) for h in range(4)]):
        pl.semaphore_signal(barrier, 1, device_id=device, device_id_type=MESH)

    @pl.when(at_end)
    def _():
        for device in (relay_to, relay_from, relay_down):
            pl.semaphore_signal(barrier, 1, device_id=device, device_id_type=MESH)

    @pl.when(at_start)
    def _():
        pl.semaphore_signal(barrier, 1, device_id=relay_up, device_id_type=MESH)

    for load in loads:
        load.wait()
    pl.semaphore_wait(barrier, 11 + 3 * (place // (ROW - 1)) + (ROW - 1 - place) // (ROW - 1))

    z1 = [remote(win.at[core, s, own_rows], win.at[core, s, hop1_rows], z1_s.at[s], z1_r.at[s], nxt) for s in stages]
    z2 = [remote(win.at[core, s, hop1_rows], win.at[core, s, hop2_rows], z2_s.at[s], z2_r.at[s], nxt) for s in stages]
    z1_relayed = remote(win.at[core, 1, own_rows], relay.at[0], z1_s.at[1], relay_r.at[0], relay_to)
    z2_relayed = remote(win.at[core, 1, hop1_rows], relay.at[1], z2_s.at[1], relay_r.at[1], relay_to)
    passed = [remote(relay.at[k], win.at[core, 1, rows], relay_s.at[k], sem.at[1], relay_down)
              for k, (rows, sem) in enumerate(((hop1_rows, z1_r), (hop2_rows, z2_r)))]
    m1 = [remote(win.at[core, s, hop1_rows], win.at[core, s, hop1_rows], m1_s.at[s], m1_r.at[s], mate)
          for s in stages]
    m1_in = [remote(win.at[other, s, hop1_rows], win.at[other, s, hop1_rows], m1_s.at[s], m1_r.at[s], mate)
             for s in stages]
    m2 = [remote(win.at[core, s, hop2_rows], win.at[core, s, hop2_rows], m2_s.at[s], m2_r.at[s], mate)
          for s in stages]
    m2_in = [remote(win.at[other, s, hop2_rows], win.at[other, s, hop2_rows], m2_s.at[s], m2_r.at[s], mate)
             for s in stages]
    xq = [[remote(ref.at[:, :, cols(1 - chip, s)], qo.at[kind, s, :, 1], x_s.at[kind, s], x_r.at[kind, s], partner)
           for kind, ref in ((0, q_ref), (1, g_ref))] for s in stages]
    mate_rows = (hop2_rows, pl.ds(TOK, 2 * TOK))
    mt = [[remote(mate_out.at[s, mate_rows[h]], mate_in.at[s, mate_rows[h]], mt_s.at[s, h], mt_r.at[s, h], mate)
           for h in halves] for s in stages]
    quarters = [pl.ds(q * 128, 128) for q in range(4)]
    r2 = [[remote(r2_out.at[s, rows], r2_in.at[s, rows], r2_s.at[s, q], r2_r.at[s, q], prv)
           for q, rows in enumerate(quarters)] for s in stages]
    r1 = [[remote(r1_out.at[s, rows], r1_in.at[s, head], r1_s.at[s, q], r1_r.at[s, head], (prv[0], q))
           for q, rows in enumerate(quarters)] for s in stages]
    r1_from = [[remote(r1_out.at[s, quarters[0]], r1_in.at[s, h], r1_s.at[s, 0], r1_r.at[s, h], prv)
                for h in range(4)] for s in stages]
    h0 = [[remote(h0_out.at[s, rows], h0_in.at[s, head], h0_s.at[s, q], h0_r.at[s, head], (ctx, q))
           for q, rows in enumerate(quarters)] for s in stages]
    h0_from = [[remote(h0_out.at[s, quarters[0]], h0_in.at[s, h], h0_s.at[s, 0], h0_r.at[s, h], mate)
                for h in range(4)] for s in stages]
    dq_far = [remote(dqs.at[s, 1], dq_ref.at[:, :, cols(chip, s)], dq_s.at[s], dq_r.at[s], partner)
              for s in stages]
    dq_far_in = [remote(dqs.at[s, 1], dq_ref.at[:, :, cols(1 - chip, s)], dq_s.at[s], dq_r.at[s], partner)
                 for s in stages]
    dq_near = [pltpu.make_async_copy(dqs.at[s, 0], dq_ref.at[:, :, cols(chip, s)], dq_l.at[s])
               for s in stages]

    z1[0].start()

    def either(direct, relayed):
        @pl.when(at_end)
        def _():
            relayed.start()

        @pl.when(jnp.logical_not(at_end))
        def _():
            direct.start()

    either(z1[1], z1_relayed)
    for copy in xq[0]:
        copy.start()

    @pl.when(jnp.logical_not(at_start | at_end))
    def _():
        for copy in xq[1]:
            copy.start()


    lengths = len_ref[...]
    upto = jnp.where(
        lax.broadcasted_iota(jnp.int32, (64, HD), 0) <= lax.broadcasted_iota(jnp.int32, (64, HD), 1), 1.0, 0.0
    ).astype(jnp.bfloat16)

    def ends_of(part):
        rows = jnp.broadcast_to(part, (16, 64)).astype(jnp.float32).astype(jnp.bfloat16)
        return mm(rows, upto)[0:1]

    ends = (ends_of(lengths >> 5) * 32.0 + ends_of(lengths & 31)).astype(jnp.int32)
    wide = (16, 64)
    before = jnp.where(
        lax.broadcasted_iota(jnp.int32, (64, HD), 0) < lax.broadcasted_iota(jnp.int32, (64, HD), 1), 1.0, 0.0
    ).astype(jnp.bfloat16)

    def starts_of(part):
        rows = jnp.broadcast_to(part, wide).astype(jnp.float32).astype(jnp.bfloat16)
        return mm(rows, before)[0:1]

    starts = (starts_of(lengths >> 5) * 32.0 + starts_of(lengths & 31)).astype(jnp.int32)
    lane = lax.broadcasted_iota(jnp.int32, (1, HD), 1)
    starts = jnp.where(lane == 64, -WIN, starts)
    ends = jnp.where(lane == 64, 0, ends)

    def inside(count, base):
        pos = lax.broadcasted_iota(jnp.int32, (count, HD), 0) + base
        return (starts <= pos) & (pos < ends)

    for t in range(0, WIN, HALF):
        key_doc[t:t + HALF] = jnp.where(inside(HALF, ctx * TOK - REACH + t), 1.0, 0.0).astype(jnp.bfloat16)
    for t in range(0, TOK, HALF):
        query_doc[t:t + HALF] = jnp.where(inside(HALF, ctx * TOK + t), 0.0, -1e30).astype(jnp.bfloat16)

    causal = (lax.broadcasted_iota(jnp.int32, (HALF, HALF), 0)
              <= lax.broadcasted_iota(jnp.int32, (HALF, HALF), 1))

    def fold(x):
        return jnp.sum(x.reshape(x.shape[0] // 8, 8, x.shape[1]), axis=0)

    slots = {(0, 0): 0, (0, 1): 2, (1, 0): 4, (1, 1): 0}

    def part(s, c, j, low, high):
        slot = slots[s, j] + c
        score, wgrad = scores.at[slot], wgrads.at[slot]
        rows = pl.ds(c * HALF + low, high - low)
        keyed = jnp.concatenate([win[0, s, rows], key_doc[rows]], axis=1)
        asked = jnp.concatenate([qo[0, s, c, j], query_doc[c * HALF:(c + 1) * HALF]], axis=1)
        score[low:high] = lax.dot_general(keyed, asked, NT, preferred_element_type=jnp.float32)
        wgrad[low:high] = lax.dot_general(
            win[1, s, rows], qo[1, s, c, j], NT, preferred_element_type=jnp.float32)
        if high == SPAN:
            score[REACH:SPAN] = jnp.where(causal, score[REACH:SPAN], -1e30)
        peak = None
        for t in range(low, high, TILE):
            x = score[t:t + TILE]
            x = jnp.max(x.reshape(TILE // 8, 8, HALF), axis=0)
            peak = x if peak is None else jnp.maximum(peak, x)
        top = jnp.max(peak, axis=0, keepdims=True)
        total = jnp.zeros((8, HALF), jnp.float32)
        dots = jnp.zeros((8, HALF), jnp.float32)
        for t in range(low, high, TILE):
            e = jnp.exp2((score[t:t + TILE] - top) * (SCALE * LOG2E))
            score[t:t + TILE] = e
            total += fold(e)
            dots += fold(e * wgrad[t:t + TILE])
        return top, jnp.sum(total, axis=0, keepdims=True), jnp.sum(dots, axis=0, keepdims=True)

    def early(s, c, j):
        slot = slots[s, j] + c
        for row, value in enumerate(part(s, c, j, TOK - c * HALF, SPAN)):
            stats[slot, row:row + 1] = value

    def late(s, c, j):
        slot, border = slots[s, j] + c, TOK - c * HALF
        score, wgrad = scores.at[slot], wgrads.at[slot]
        far_top, far_total, far_dots = part(s, c, j, 0, border)
        near_top, near_total, near_dots = (stats[slot, row:row + 1] for row in range(3))
        top = jnp.maximum(far_top, near_top)
        far_scale = jnp.exp2((far_top - top) * (SCALE * LOG2E))
        near_scale = jnp.exp2((near_top - top) * (SCALE * LOG2E))
        inverse = 1.0 / (far_total * far_scale + near_total * near_scale)
        delta = (far_dots * far_scale + near_dots * near_scale) * inverse
        at = pl.ds(c * TOK + j * HALF, HALF)
        for t in range(0, SPAN, TILE):
            weights = score[t:t + TILE] * ((far_scale if t < border else near_scale) * inverse)
            rows = slice(c * HALF + t, c * HALF + t + TILE)
            pd[s, 1, rows, at] = weights.astype(jnp.bfloat16)
            pd[s, 0, rows, at] = (weights * (wgrad[t:t + TILE] - delta)).astype(jnp.bfloat16)

    def query_grads(s):
        for c in halves:
            rows = pl.ds(c * HALF, SPAN)
            found = lax.dot_general(
                pd[s, 0, rows, c * TOK:(c + 1) * TOK], win[0, s, rows], TN, preferred_element_type=jnp.float32)
            dqs[s, :, c] = (found * SCALE).astype(jnp.bfloat16).reshape(2, HALF, HD)
        dq_far[s].start()
        dq_near[s].start()

    pieces = (((0, HALF, 0, 1), (HALF, TOK, 0, 2)), ((TOK, SPAN, 0, 2), (SPAN, WIN, 1, 2)))

    def product(kind, s, piece):
        low, high, c0, c1 = piece
        right = qo[kind, s, c0:c1].reshape(((c1 - c0) * TOK, HD))
        return mm(pd[s, kind, low:high, c0 * TOK:c1 * TOK], right) * jnp.where(kind == 0, SCALE, 1.0)

    def theirs(s, h):
        for piece in pieces[h]:
            mate_out[s, piece[0]:piece[1]] = product(other, s, piece).astype(jnp.bfloat16)
        mt[s][h].start()

    def ours(s, h):
        for piece in pieces[h]:
            mine[piece[0]:piece[1]] = product(core, s, piece)

    def outer(s):
        theirs(s, 0)
        ours(s, 0)
        theirs(s, 1)
        mt[s][0].wait_recv()
        for q in range(4):
            at = slice(q * 128, (q + 1) * 128)
            r2_out[s, at] = (mine[at] + mate_in[s, at].astype(jnp.float32)).astype(jnp.bfloat16)
            r2[s][q].start()
        ours(s, 1)
        mt[s][1].wait_recv()
        hop1[s] = mine[TOK:REACH] + mate_in[s, TOK:REACH].astype(jnp.float32)
        h0_out[s] = (mine[REACH:WIN] + mate_in[s, REACH:WIN].astype(jnp.float32)).astype(jnp.bfloat16)
        for q in range(4):
            @pl.when(head != q)
            def _(q=q):
                h0[s][q].start()

            @pl.when(head == q)
            def _(q=q):
                pltpu.make_async_copy(h0_out.at[s, quarters[q]], h0_in.at[s, q], h0_r.at[s, q]).start()

    def middle(s):
        for q in range(4):
            at = slice(q * 128, (q + 1) * 128)
            r2[s][q].wait_recv()
            r1_out[s, at] = (hop1[s, at] + r2_in[s, at].astype(jnp.float32)).astype(jnp.bfloat16)
            r1[s][q].start()

    def finish(s):
        for h in range(4):
            h0_from[s][h].wait_recv()
            r1_from[s][h].wait_recv()
            out = (dk_ref, dv_ref)[h % 2]
            g = (h // 2) * 2 + s
            out[:, g * HD:(g + 1) * HD] = (
                h0_in[s, h].astype(jnp.float32) + r1_in[s, h].astype(jnp.float32)).astype(jnp.bfloat16)

    def forward(s):
        z1[s].wait_recv()
        if s == 1:
            either(z2[1], z2_relayed)
        else:
            z2[s].start()
        m1[s].start()

    def pass_on(k):
        @pl.when(at_end)
        def _():
            (z1_relayed, z2_relayed)[k].wait_recv()
            passed[k].start()

    def arrive(s):
        z2[s].wait_recv()
        m2[s].start()

    forward(0)
    m1_in[0].wait_recv()
    early(0, 0, 0)
    early(0, 1, 0)

    @pl.when(jnp.logical_not(at_start))
    def _():
        forward(1)

    pass_on(0)

    @pl.when(jnp.logical_not(at_start))
    def _():
        m1_in[1].wait_recv()
        early(1, 0, 0)
        early(1, 1, 0)

    for copy in xq[0]:
        copy.wait_recv()

    @pl.when(at_start | at_end)
    def _():
        for copy in xq[1]:
            copy.start()

    early(0, 0, 1)
    arrive(0)
    early(0, 1, 1)
    m2_in[0].wait_recv()
    late(0, 0, 0)

    @pl.when(at_start)
    def _():
        forward(1)

    pass_on(1)
    late(0, 1, 0)
    late(0, 0, 1)
    late(0, 1, 1)
    outer(0)

    @pl.when(at_start)
    def _():
        m1_in[1].wait_recv()
        early(1, 0, 0)
        early(1, 1, 0)

    arrive(1)
    query_grads(0)
    m2_in[1].wait_recv()
    late(1, 0, 0)
    late(1, 1, 0)
    middle(0)
    for copy in xq[1]:
        copy.wait_recv()
    early(1, 0, 1)
    late(1, 0, 1)
    early(1, 1, 1)
    late(1, 1, 1)
    outer(1)
    query_grads(1)
    finish(0)
    middle(1)
    finish(1)

    @pl.when(at_end)
    def _():
        for copy in passed:
            copy.wait_send()

    for s in stages:
        for copy in (z1[s], z2[s], m1[s], m2[s], *xq[s], *mt[s], *r2[s], *r1[s], dq_far[s]):
            copy.wait_send()
        for q in range(4):
            @pl.when(head != q)
            def _(q=q):
                h0[s][q].wait_send()
        dq_far_in[s].wait_recv()
        dq_near[s].wait()


def write_out(*refs):
    sources, targets, sem = refs[0:3], refs[3:6], refs[6]
    copies = [pltpu.make_async_copy(source, target, sem.at[i])
              for i, (source, target) in enumerate(zip(sources, targets, strict=True))]
    for copy in copies:
        copy.start()
    for copy in copies:
        copy.wait()


def local(ctx_size, queries, keys, values, grad_out, doc_lengths):
    bf16, f32 = jnp.bfloat16, jnp.float32
    anywhere = pl.BlockSpec(memory_space=pl.ANY)
    pair = pltpu.SemaphoreType.DMA((STAGES,))
    quad = pltpu.SemaphoreType.DMA((STAGES, 2))
    eight = pltpu.SemaphoreType.DMA((STAGES, 4))
    block16 = pltpu.VMEM((STAGES, TOK, HD), bf16)
    heads16 = pltpu.VMEM((STAGES, 4, 128, HD), bf16)
    dq, dk, dv = pl.pallas_call(
        lambda *refs: kernel(ctx_size, *refs),
        out_shape=(
            pltpu.VMEM((2, HALF, KVH * HD), bf16),
            pltpu.VMEM((128, KVH * HD), bf16),
            pltpu.VMEM((128, KVH * HD), bf16),
        ),
        in_specs=[anywhere] * 4 + [pl.BlockSpec(memory_space=pltpu.VMEM)],
        out_specs=(pl.BlockSpec(memory_space=pltpu.VMEM), pl.BlockSpec(memory_space=pltpu.VMEM), pl.BlockSpec(memory_space=pltpu.VMEM)),
        scratch_shapes=[
            pltpu.VMEM((2, STAGES, WIN, HD), bf16),
            pltpu.VMEM((2, STAGES, 2, 2, HALF, HD), bf16),
            pltpu.VMEM((STAGES, 2, WIN, 2 * TOK), bf16),
            pltpu.VMEM((6, SPAN, HALF), f32),
            pltpu.VMEM((6, SPAN, HALF), f32),
            pltpu.VMEM((6, 8, HALF), f32),
            pltpu.VMEM((WIN, HD), f32),
            pltpu.VMEM((STAGES, 2, 2, HALF, HD), bf16),
            pltpu.VMEM((WIN, HD), bf16),
            pltpu.VMEM((TOK, HD), bf16),
            pltpu.VMEM((STAGES, WIN, HD), bf16),
            pltpu.VMEM((STAGES, WIN, HD), bf16),
            pltpu.VMEM((STAGES, TOK, HD), f32),
            block16, block16, block16, heads16, block16, heads16,
            block16,
            pltpu.SemaphoreType.DMA((4, STAGES)),
            pair, pair, pair, pair, pair, pair, pair, pair,
            quad, quad,
            quad, quad, eight, eight, eight, eight, pair, pair, pair,
            eight, eight,
            pair, pair,
        ],
        compiler_params=pltpu.CompilerParams(
            collective_id=0, has_side_effects=True, vmem_limit_bytes=56 * 2**20),
        cost_estimate=pl.CostEstimate(
            flops=10 * 4 * TOK * SPAN * HD, bytes_accessed=4 * 2**20, transcendentals=4 * TOK * SPAN),
        name="attention_backward",
    )(queries.reshape(2, HALF, KVH * HD), keys, values, grad_out.reshape(2, HALF, KVH * HD),
      doc_lengths.reshape(1, 64))
    dq, dk, dv = pl.pallas_call(
        write_out,
        out_shape=tuple(jax.ShapeDtypeStruct(x.shape, bf16) for x in (dq, dk, dv)),
        in_specs=[anywhere] * 3,
        out_specs=(anywhere,) * 3,
        scratch_shapes=[pltpu.SemaphoreType.DMA((3,))],
        compiler_params=pltpu.CompilerParams(vmem_limit_bytes=4 * 2**20),
        name="write_out",
    )(dq, dk, dv)
    return dq.reshape(TOK, 1, KVH * HD), dk, dv


def solution(mesh):
    placed = (P("ctx", "head", None), P("ctx", None), P("ctx", None), P("ctx", "head", None), P())
    ctx_size = mesh.shape["ctx"]
    return jax.shard_map(
        lambda *args: local(ctx_size, *args),
        mesh=mesh,
        in_specs=placed,
        out_specs=(P("ctx", "head", None), P(("ctx", "head"), None), P(("ctx", "head"), None)),
        check_vma=False,
    )
```
